256 devices in a mesh: tile: 8 (over z), text: 32 (over y, x, core).
Axes of the slice: x: 4, y: 4, z: 8, core: 2. Of those that a mesh axis runs over, the one named last changes fastest.
Arguments:
- grad_seq: bfloat16 [10240, 8192], P('text', 'tile'), may hold values from -6 to 6
- positions: int32 [10240], replicated, may hold values from 0 to 10239, each once
- pre_act: bfloat16 [10240, 5120], P('tile', 'text'), may hold values from -6 to 6
- w_out: bfloat16 [5120, 8192], P('text', 'tile'), may hold values from -0.078125 to 0.078125
Outputs:
- grad_pre: float32 [10240, 5120], P('tile', 'text')
- grad_w_out: float32 [5120, 8192], P('text', 'tile')
- grad_bias: float32 [8192], P('tile')
The draws below stay inside these ranges and needn't reach their ends.
Inputs may be any that keep to these rules, and one draw needn't show every extreme that they name: positions names every place 0 to 10239 once.
All inputs are finite; a program needn't handle non-finite values.
Results may differ from the reference program's by a relative error of at most 0.003.
Values may be sent and summed in bfloat16 or wider, within the bound.
No kernel may reach another device: no remote copies, remote signals or barrier semaphores. Data moves between devices by JAX's collectives and lax.ppermute only.
A program may use at most 128 MiB of HBM per device.

```python
import jax
import jax.numpy as jnp
from jax import lax

DM = 5120
OUT = 8192
SLOTS = 10240
N_TILE = 8


def spiked(array, rng, source, target, blocks, factor):
    owner, partner = [(jnp.arange(array.shape[position]) // (array.shape[position] // blocks)).reshape([-1 if axis == position else 1 for axis in range(array.ndim)]) for position in (source, target)]
    chosen = jax.random.permutation(rng, blocks)[partner]
    strong = (owner == chosen) | (owner == (partner + blocks // 2) % blocks)
    return jnp.where(strong, factor * array, array)


def steps_of(rng, dims, pieces, least, high):
    loudness = 1.0
    for dim, parts in pieces:
        draws = jax.random.uniform(jax.random.fold_in(jax.random.fold_in(rng, 6), dim), (parts,), jnp.float32, least / len(pieces), high / len(pieces))
        loudness = loudness * jnp.repeat(jnp.exp(draws), dims[dim] // parts).reshape((-1,) + (1,) * (len(dims) - 1 - dim))
    return loudness


def normal_values(key, extent, scale, bound, cuts=(), kind=jnp.bfloat16):
    loudness = steps_of(key, extent, cuts, -0.22, 0.18) if cuts else 1.0
    array = jax.random.normal(key, extent, jnp.float32) * scale * loudness
    return jnp.minimum(jnp.maximum(array, -bound), bound).astype(kind)


def noise_with(key, extent, scale, reach, cuts, heavy, held_as=jnp.bfloat16):
    drawn = scale * jax.random.normal(key, extent, jnp.float32)
    if cuts:
        drawn = drawn * steps_of(key, extent, cuts, -0.22, 0.18)
    return jnp.clip(spiked(drawn, jax.random.fold_in(key, 3), *heavy), -reach, reach).astype(held_as)


def setup_inputs(seed: int = 0) -> dict:
    key_list = jax.random.split(jax.random.key(seed), 5)
    return {
        "grad_seq": noise_with(key_list[0], (SLOTS, OUT), 1.0, 6.0, ((0, 32), (1, 8)), (0, 1, 32, 2.75)),
        "positions": jax.random.permutation(key_list[1], SLOTS).astype(jnp.int32),
        "pre_act": normal_values(key_list[2], (SLOTS, DM), 1.0, 6.0, ((0, 8), (1, 32))),
        "w_out": normal_values(key_list[3], (DM, OUT), DM ** -0.5, 0.078125, ((0, 32), (1, 8))),
    }


def gelu_parts(pre):
    value = pre.astype(jnp.float32)
    cdf = 0.5 * (1.0 + jax.scipy.special.erf(value * 0.7071067811865476))
    activated = value * cdf
    slope = cdf + value * jnp.exp(-0.5 * value * value) * 0.3989422804014327
    return activated, slope


def reference(grad_seq, positions, pre_act, w_out):
    slot_grad = jnp.take(grad_seq, positions.astype(jnp.int32), axis=0)
    activated, slope = gelu_parts(pre_act)
    act_bf = activated.astype(jnp.bfloat16)
    width = OUT // N_TILE

    def add_block(total, block_index):
        start = (block_index * width).astype(jnp.int32)
        grad_block = lax.dynamic_slice_in_dim(slot_grad, start, width, 1)
        weight_block = lax.dynamic_slice_in_dim(w_out, start, width, 1)
        partial_term = jnp.dot(grad_block, weight_block.T, preferred_element_type=jnp.float32)
        return total + partial_term, None

    start_total = jnp.zeros((slot_grad.shape[0], w_out.shape[0]), jnp.float32)
    grad_act, _ = lax.scan(add_block, start_total, jnp.arange(N_TILE, dtype=jnp.int32))
    grad_pre = grad_act * slope
    grad_w_out = jnp.dot(act_bf.T, slot_grad, preferred_element_type=jnp.float32)
    grad_bias = jnp.sum(grad_seq.astype(jnp.float32), axis=0)
    return grad_pre, grad_w_out, grad_bias
```

```python
import jax
import jax.numpy as jnp
from jax import lax
from jax.experimental import pallas as pl
from jax.experimental.pallas import tpu as pltpu
from jax.sharding import PartitionSpec as P

SIDE = 4
N_TEXT = 2 * SIDE * SIDE
N_TILE = 8
ROWS = 320
HID = 160
BLOCK = 1280
SLOTS = 10240
WIDTH = 1024
ONES = 16
HALF = HID // 2
F32 = jnp.float32
BF16 = jnp.bfloat16


def plane_perm(step0, step1):
    pairs = []
    for y in range(SIDE):
        for x in range(SIDE):
            for core, (dy, dx) in ((0, step0), (1, step1)):
                target = (((y + dy) % SIDE) * SIDE + (x + dx) % SIDE) * 2 + core
                pairs.append(((y * SIDE + x) * 2 + core, target))
    return pairs


FIRST_UP = plane_perm((0, 1), (1, 0))
FIRST_DOWN = plane_perm((0, -1), (-1, 0))
SECOND_UP = plane_perm((1, 0), (0, 1))
SECOND_DOWN = plane_perm((-1, 0), (0, -1))
SWAP = [(i, i ^ 1) for i in range(N_TEXT)]
TILE_UP = [(i, (i + 1) % N_TILE) for i in range(N_TILE)]
TILE_DOWN = [(i, (i - 1) % N_TILE) for i in range(N_TILE)]


def gather_pieces(grad):
    send = lambda value, perm: lax.ppermute(value, "text", perm)
    near, far_side = send(grad, FIRST_UP), send(grad, FIRST_DOWN)
    row = [grad, near, send(near, FIRST_UP), far_side]
    up = [send(piece, SECOND_UP) for piece in row]
    down = [send(piece, SECOND_DOWN) for piece in row]
    far = [send(up[0], SECOND_UP), send(up[1], SECOND_UP), send(down[2], SECOND_DOWN), send(down[3], SECOND_DOWN)]
    pieces = []
    for group in (row, up, down, far):
        pieces += group + [send(piece, SWAP) for piece in group]
    return pieces


def arrival_place(device, me):
    core, x, y = device & 1, (device >> 1) & 3, device >> 3
    my_core, my_x, my_y = me & 1, (me >> 1) & 3, me >> 3
    dx, dy = (my_x - x) & 3, (my_y - y) & 3
    first = jnp.where(core == 0, dx, dy)
    second = jnp.where(core == 0, dy, dx)
    return (second ^ (second >> 1)) * 8 + (core ^ my_core) * 4 + first


def act_kernel(place_ref, act_ref, out_ref, rows, turned):
    block = pl.program_id(0)
    turned[...] = act_ref[0].astype(F32).T

    @pl.loop(0, BLOCK, step=16)
    def _(start):
        for i in range(16):
            where = place_ref[block * BLOCK + start + i]
            rows[pl.ds(where, 1), :] = turned[pl.ds(start + i, 1), :]

    @pl.when(block == N_TILE - 1)
    def _():
        @pl.loop(0, N_TEXT)
        def _(k):
            out_ref[k, 0:HID, :] = rows[pl.ds(pl.multiple_of(k * ROWS, 64), ROWS), :].T.astype(BF16)
            out_ref[k, HID:HID + ONES, :] = jnp.ones((ONES, ROWS), BF16)


def act_in_arrival_order(place, act):
    return pl.pallas_call(
        act_kernel,
        out_shape=jax.ShapeDtypeStruct((N_TEXT, HID + ONES, ROWS), BF16),
        grid_spec=pltpu.PrefetchScalarGridSpec(
            num_scalar_prefetch=1,
            grid=(N_TILE,),
            in_specs=[pl.BlockSpec((1, HID, BLOCK), lambda i, place: (i, 0, 0))],
            out_specs=pl.BlockSpec((N_TEXT, HID + ONES, ROWS), lambda i, place: (0, 0, 0)),
            scratch_shapes=[pltpu.VMEM((SLOTS, HID), F32), pltpu.VMEM((BLOCK, HID), F32)],
        ),
        compiler_params=pltpu.CompilerParams(vmem_limit_bytes=28 * 2**20),
        cost_estimate=pl.CostEstimate(flops=0, bytes_accessed=40_000_000, transcendentals=0),
        name="act_rows",
    )(place, act)


def slot_kernel(count, place_ref, blocks_ref, *refs):
    pieces, (out_ref, rows, picked, sems) = refs[:N_TEXT], refs[N_TEXT:]
    copies = [
        pltpu.make_async_copy(piece, rows.at[pl.ds(k * ROWS, ROWS), :], sems.at[k]) for k, piece in enumerate(pieces)
    ]
    for copy in copies:
        copy.start()
    for copy in copies:
        copy.wait()

    @pl.loop(0, count)
    def _(b):
        base = blocks_ref[b] * BLOCK

        @pl.loop(0, BLOCK, step=16)
        def _(start):
            for i in range(16):
                where = place_ref[base + start + i]
                picked[pl.ds(start + i, 1), :] = rows[pl.ds(where, 1), :]

        out_ref[b] = picked[...].T


def to_slot_order(place, blocks, pieces):
    count = blocks.shape[0]
    return pl.pallas_call(
        lambda *refs: slot_kernel(count, *refs),
        out_shape=jax.ShapeDtypeStruct((count, HID, BLOCK), F32),
        in_specs=[pl.BlockSpec(memory_space=pltpu.SMEM)] * 2 + [pl.BlockSpec(memory_space=pl.ANY)] * N_TEXT,
        out_specs=pl.BlockSpec(memory_space=pltpu.VMEM),
        scratch_shapes=[
            pltpu.VMEM((SLOTS, HID), F32),
            pltpu.VMEM((BLOCK, HID), F32),
            pltpu.SemaphoreType.DMA((N_TEXT,)),
        ],
        compiler_params=pltpu.CompilerParams(vmem_limit_bytes=28 * 2**20),
        cost_estimate=pl.CostEstimate(flops=0, bytes_accessed=8_000_000 + 5_000_000 * count, transcendentals=0),
        name="slot_rows",
    )(place, blocks, *pieces)


def weight_kernel(order_ref, act_ref, *refs):
    pieces, (out_ref, bias_ref, held, sums, sems) = refs[:N_TEXT], refs[N_TEXT:]
    copies = [pltpu.make_async_copy(piece, held.at[k], sems.at[k]) for k, piece in enumerate(pieces)]
    for copy in copies:
        copy.start()
    for copy in copies:
        copy.wait()
    out_ref[...] = jnp.zeros_like(out_ref)

    @pl.loop(0, N_TEXT)
    def _(k):
        term = jnp.dot(act_ref[k], held[k], preferred_element_type=F32)
        out_ref[...] += term[:HID]
        sums[pl.ds(order_ref[k], 1), :] = term[HID:HID + 1]

    bias_ref[...] = jnp.sum(sums[...], axis=0, keepdims=True)


def weight_gradient(order, act, pieces):
    return pl.pallas_call(
        weight_kernel,
        out_shape=(jax.ShapeDtypeStruct((HID, WIDTH), F32), jax.ShapeDtypeStruct((1, WIDTH), F32)),
        in_specs=[pl.BlockSpec(memory_space=pltpu.SMEM), pl.BlockSpec(memory_space=pltpu.VMEM)]
        + [pl.BlockSpec(memory_space=pl.ANY)] * N_TEXT,
        out_specs=[pl.BlockSpec(memory_space=pltpu.VMEM)] * 2,
        scratch_shapes=[
            pltpu.VMEM((N_TEXT, ROWS, WIDTH), BF16),
            pltpu.VMEM((N_TEXT, WIDTH), F32),
            pltpu.SemaphoreType.DMA((N_TEXT,)),
        ],
        compiler_params=pltpu.CompilerParams(vmem_limit_bytes=32 * 2**20),
        cost_estimate=pl.CostEstimate(flops=5_000_000_000, bytes_accessed=30_000_000, transcendentals=0),
        name="weight_gradient",
    )(order, act, *pieces)


def gelu_parts(pre):
    value = pre.astype(F32)
    cdf = 0.5 * (1.0 + jax.scipy.special.erf(value * 0.7071067811865476))
    activated = value * cdf
    slope = cdf + value * jnp.exp(-0.5 * value * value) * 0.3989422804014327
    return activated, slope


def body(grad_seq, positions, pre_act, w_out):
    me, tile = lax.axis_index("text"), lax.axis_index("tile")
    place = arrival_place(positions // ROWS, me) * ROWS + positions % ROWS
    piece_of = arrival_place(jnp.arange(N_TEXT, dtype=jnp.int32), me)
    order = jnp.argmax(piece_of[None, :] == jnp.arange(N_TEXT, dtype=jnp.int32)[:, None], axis=1).astype(jnp.int32)

    pre = pre_act.T
    pre_all = lax.all_gather(pre, "tile", axis=0)
    pieces = gather_pieces(grad_seq)
    act_all = gelu_parts(pre_all)[0].astype(BF16)
    act = act_in_arrival_order(place, act_all)

    products = [jnp.einsum("ro,ho->rh", piece, w_out, preferred_element_type=F32) for piece in pieces]
    early = to_slot_order(place, (tile + jnp.array([4, 3, 5], jnp.int32)) % N_TILE, products)
    late = to_slot_order(place, (tile + jnp.array([2, 6, 1, 7, 0], jnp.int32)) % N_TILE, products)
    across, up3, down3 = early[0], early[1], early[2]
    up2, down2, up1, down1, own = (late[i] for i in range(5))
    low, high = slice(0, HALF), slice(HALF, HID)

    def ring(perm, terms):
        run = terms[0].astype(BF16)
        for term in terms[1:]:
            run = (lax.ppermute(run, "tile", perm).astype(F32) + term).astype(BF16)
        return lax.ppermute(run, "tile", perm).astype(F32)

    low_sum = ring(TILE_UP, [t[low] for t in (across, up3, up2, up1)]) + ring(
        TILE_DOWN, [t[low] for t in (down3, down2, down1)]
    )
    high_sum = ring(TILE_DOWN, [t[high] for t in (across, down3, down2, down1)]) + ring(
        TILE_UP, [t[high] for t in (up3, up2, up1)]
    )
    grad_pre = (own + jnp.concatenate([low_sum, high_sum], axis=0)) * gelu_parts(pre)[1]
    grad_w, bias = weight_gradient(order, act, pieces)
    return grad_pre.T, grad_w, bias[0]


def solution(mesh):
    in_specs = (P("text", "tile"), P(), P("tile", "text"), P("text", "tile"))
    out_specs = (P("tile", "text"), P("text", "tile"), P("tile"))
    return jax.shard_map(body, mesh=mesh, in_specs=in_specs, out_specs=out_specs, check_vma=False)
```

```python
import functools

import jax
import jax.numpy as jnp
from jax import lax
from jax.experimental import pallas as pl
from jax.experimental.pallas import tpu as pltpu
from jax.sharding import PartitionSpec as P

SIDE = 4
N_TEXT = 2 * SIDE * SIDE
N_TILE = 8
ROWS = 320
HID = 160
BLOCK = 1280
SLOTS = 10240
WIDTH = 1024
HALF = HID // 2
LANES = 128
GROUPS = 4
GROUP_ROWS = 4 * ROWS
UNROLL = 32
F32 = jnp.float32
BF16 = jnp.bfloat16


def plane_perm(step0, step1):
    pairs = []
    for y in range(SIDE):
        for x in range(SIDE):
            for core, (dy, dx) in ((0, step0), (1, step1)):
                target = (((y + dy) % SIDE) * SIDE + (x + dx) % SIDE) * 2 + core
                pairs.append(((y * SIDE + x) * 2 + core, target))
    return pairs


FIRST_UP = plane_perm((0, 1), (1, 0))
FIRST_DOWN = plane_perm((0, -1), (-1, 0))
SECOND_UP = plane_perm((1, 0), (0, 1))
SECOND_DOWN = plane_perm((-1, 0), (0, -1))
SWAP = [(i, i ^ 1) for i in range(N_TEXT)]
TILE_UP = [(i, (i + 1) % N_TILE) for i in range(N_TILE)]
TILE_DOWN = [(i, (i - 1) % N_TILE) for i in range(N_TILE)]


def gather_pieces(grad):
    send = lambda value, perm: lax.ppermute(value, "text", perm)
    near, far_side = send(grad, FIRST_UP), send(grad, FIRST_DOWN)
    row = [grad, near, send(near, FIRST_UP), far_side]
    up = [send(piece, SECOND_UP) for piece in row]
    down = [send(piece, SECOND_DOWN) for piece in row]
    far = [send(up[0], SECOND_UP), send(up[1], SECOND_UP), send(down[2], SECOND_DOWN), send(down[3], SECOND_DOWN)]
    return row, up, down, far


def arrival_place(device, me):
    core, x, y = device & 1, (device >> 1) & 3, device >> 3
    my_core, my_x, my_y = me & 1, (me >> 1) & 3, me >> 3
    dx, dy = (my_x - x) & 3, (my_y - y) & 3
    first = jnp.where(core == 0, dx, dy)
    second = jnp.where(core == 0, dy, dx)
    return (core ^ my_core) * 16 + (second ^ (second >> 1)) * 4 + first


def store_rows(ref, start, value):
    count = value.shape[0]
    ref[pl.ds(start, count, stride=2), :] = value[:, :LANES]
    ref[pl.ds(start + 1, count, stride=2), 0:HID - LANES] = value[:, LANES:]


def load_turned(ref, start, count):
    left = ref[pl.ds(start, count, stride=2), :].T
    right = ref[pl.ds(start + 1, count, stride=2), :].T
    return left, right[0:HID - LANES]


def act_kernel(place_ref, act_ref, mine_ref, theirs_ref, rows, turned):
    block = pl.program_id(0)
    store_rows(turned, 0, act_ref[0].astype(F32).T)

    @pl.loop(0, BLOCK, step=UNROLL)
    def _(start):
        held = [turned[pl.ds(pl.multiple_of(2 * start, 2) + 2 * i, 2), :] for i in range(UNROLL)]
        for i in range(UNROLL):
            where = pl.multiple_of(place_ref[block * BLOCK + start + i], 2)
            rows[pl.ds(where, 2), :] = held[i]

    @pl.when(block == N_TILE - 1)
    def _():
        for group in range(2 * GROUPS):
            left, right = load_turned(rows, group * 2 * GROUP_ROWS, GROUP_ROWS)
            out_ref = (mine_ref, theirs_ref)[group // GROUPS]
            out_ref[group % GROUPS, 0:LANES, :] = left.astype(BF16)
            out_ref[group % GROUPS, LANES:HID, :] = right.astype(BF16)


def act_in_arrival_order(place, act):
    return pl.pallas_call(
        act_kernel,
        out_shape=[jax.ShapeDtypeStruct((GROUPS, HID, GROUP_ROWS), BF16)] * 2,
        grid_spec=pltpu.PrefetchScalarGridSpec(
            num_scalar_prefetch=1,
            grid=(N_TILE,),
            in_specs=[pl.BlockSpec((1, HID, BLOCK), lambda i, place: (i, 0, 0))],
            out_specs=[pl.BlockSpec((GROUPS, HID, GROUP_ROWS), lambda i, place: (0, 0, 0))] * 2,
            scratch_shapes=[pltpu.VMEM((2 * SLOTS, LANES), F32), pltpu.VMEM((2 * BLOCK, LANES), F32)],
        ),
        compiler_params=pltpu.CompilerParams(vmem_limit_bytes=20 * 2**20),
        cost_estimate=pl.CostEstimate(flops=0, bytes_accessed=70_000_000, transcendentals=0),
        name="act_rows",
    )(place, act)


def product_kernel(weight_ref, *refs):
    pieces, (mine_ref, theirs_ref, sums_ref) = refs[:4], refs[-3:]
    for k in range(4):
        piece = pieces[k][...]
        term = lax.dot_general(piece, weight_ref[...], (((1,), (1,)), ((), ())), preferred_element_type=F32)
        store_rows(mine_ref, 2 * k * ROWS, term[:, :HID])
        store_rows(theirs_ref, 2 * k * ROWS, term[:, HID:])
        sums_ref[k:k + 1, :] = jnp.sum(piece.astype(F32), axis=0, keepdims=True)


def products_of(weight, pieces, after):
    vmem = pl.BlockSpec(memory_space=pltpu.VMEM)
    half = jax.ShapeDtypeStruct((2 * GROUP_ROWS, LANES), F32)
    return pl.pallas_call(
        product_kernel,
        out_shape=(half, half, jax.ShapeDtypeStruct((4, WIDTH), F32)),
        in_specs=[vmem] * 5 + [pl.BlockSpec(memory_space=pl.ANY)] * len(after),
        out_specs=[vmem] * 3,
        compiler_params=pltpu.CompilerParams(vmem_limit_bytes=6 * 2**20),
        cost_estimate=pl.CostEstimate(flops=1_300_000_000, bytes_accessed=8_000_000, transcendentals=0),
        name="products",
    )(weight, *pieces, *after)


def slot_kernel(count, place_ref, blocks_ref, *refs):
    out_ref, picked = refs[-2:]
    if len(refs) == 3:
        rows_ref = refs[0]
    else:
        rows_ref = refs[8]
        for k in range(8):
            rows_ref[k * 2 * GROUP_ROWS:(k + 1) * 2 * GROUP_ROWS, :] = refs[k][...]

    @pl.loop(0, count)
    def _(b):
        base = blocks_ref[b] * BLOCK

        @pl.loop(0, BLOCK, step=UNROLL)
        def _(start):
            held = []
            for i in range(UNROLL):
                where = pl.multiple_of(place_ref[base + start + i], 2)
                held.append(rows_ref[pl.ds(where, 2), :])
            for i in range(UNROLL):
                picked[pl.ds(pl.multiple_of(2 * start, 2) + 2 * i, 2), :] = held[i]

        left, right = load_turned(picked, 0, BLOCK)
        out_ref[b, 0:LANES, :] = left
        out_ref[b, LANES:HID, :] = right


def to_slot_order(place, blocks, rows):
    count = blocks.shape[0]
    vmem = pl.BlockSpec(memory_space=pltpu.VMEM)
    out = [jax.ShapeDtypeStruct((count, HID, BLOCK), F32)]
    if len(rows) > 1:
        out.insert(0, jax.ShapeDtypeStruct((2 * SLOTS, LANES), F32))
    return pl.pallas_call(
        functools.partial(slot_kernel, count),
        out_shape=out,
        in_specs=[pl.BlockSpec(memory_space=pltpu.SMEM)] * 2 + [vmem] * len(rows),
        out_specs=[vmem] * len(out),
        scratch_shapes=[pltpu.VMEM((2 * BLOCK, LANES), F32)],
        compiler_params=pltpu.CompilerParams(vmem_limit_bytes=5 * 2**20),
        cost_estimate=pl.CostEstimate(flops=0, bytes_accessed=8_000_000 * count, transcendentals=0),
        name="slot_rows",
    )(place, blocks, *rows)


def weight_kernel(first, mine_ref, theirs_ref, *refs):
    pieces = refs[:4]
    out_mine, out_theirs, held, sems = refs[-4:]
    copies = [
        pltpu.make_async_copy(piece, held.at[pl.ds(k * ROWS, ROWS), :], sems.at[k]) for k, piece in enumerate(pieces)
    ]
    for copy in copies:
        copy.start()
    for copy in copies:
        copy.wait()
    act = jnp.concatenate([mine_ref[...], theirs_ref[...]], axis=0)
    for n in range(0, WIDTH, 256):
        columns = slice(n, n + 256)
        term = jnp.dot(act, held[:, columns], preferred_element_type=F32)
        out_mine[:, columns] = term[:HID] if first else refs[4][:, columns] + term[:HID]
        out_theirs[:, columns] = term[HID:] if first else refs[5][:, columns] + term[HID:]


def weight_term(mine, theirs, pieces, totals):
    vmem = pl.BlockSpec(memory_space=pltpu.VMEM)
    return pl.pallas_call(
        functools.partial(weight_kernel, not totals),
        out_shape=[jax.ShapeDtypeStruct((HID, WIDTH), F32)] * 2,
        in_specs=[vmem] * 2 + [pl.BlockSpec(memory_space=pl.ANY)] * 4 + [vmem] * len(totals),
        out_specs=[vmem] * 2,
        scratch_shapes=[pltpu.VMEM((GROUP_ROWS, WIDTH), BF16), pltpu.SemaphoreType.DMA((4,))],
        compiler_params=pltpu.CompilerParams(vmem_limit_bytes=6 * 2**20),
        cost_estimate=pl.CostEstimate(flops=1_300_000_000, bytes_accessed=8_000_000, transcendentals=0),
        name="weight_term",
    )(mine, theirs, *pieces, *totals)


def gelu_parts(pre):
    value = pre.astype(F32)
    cdf = 0.5 * (1.0 + jax.scipy.special.erf(value * 0.7071067811865476))
    activated = value * cdf
    slope = cdf + value * jnp.exp(-0.5 * value * value) * 0.3989422804014327
    return activated, slope


def body(grad_seq, positions, pre_act, w_out):
    me, tile = lax.axis_index("text"), lax.axis_index("tile")
    place = 2 * (arrival_place(positions // ROWS, me) * ROWS + positions % ROWS)
    piece_of = arrival_place(jnp.arange(N_TEXT, dtype=jnp.int32), me)

    activated, slope = gelu_parts(pre_act.T)
    act_all = lax.all_gather(activated.astype(BF16), "tile", axis=0)
    swap = lambda value: lax.ppermute(value, "text", SWAP)
    groups = gather_pieces(grad_seq)
    weight = jnp.concatenate([w_out, swap(w_out)], axis=0)
    act_mine, act_theirs = act_in_arrival_order(place, act_all)
    act_theirs = swap(act_theirs)

    mine, theirs, sums = [], [], []
    for g in range(GROUPS):
        kept, sent, part = products_of(weight, groups[g], [act_mine] if g == GROUPS - 1 else [])
        mine.append(kept)
        theirs.append(swap(sent))
        sums.append(part)
    rows, early = to_slot_order(place, (tile + jnp.array([4, 3, 5], jnp.int32)) % N_TILE, mine + theirs)
    (late,) = to_slot_order(place, (tile + jnp.array([2, 6, 1, 7, 0], jnp.int32)) % N_TILE, [rows])
    across, up3, down3 = early[0], early[1], early[2]
    up2, down2, up1, down1, own = (late[i] for i in range(5))
    low, high = slice(0, HALF), slice(HALF, HID)

    def ring(perm, terms):
        run = terms[0].astype(BF16)
        for term in terms[1:]:
            run = (lax.ppermute(run, "tile", perm).astype(F32) + term).astype(BF16)
        return lax.ppermute(run, "tile", perm).astype(F32)

    low_sum = ring(TILE_UP, [t[low] for t in (across, up3, up2, up1)]) + ring(
        TILE_DOWN, [t[low] for t in (down3, down2, down1)]
    )
    high_sum = ring(TILE_DOWN, [t[high] for t in (across, down3, down2, down1)]) + ring(
        TILE_UP, [t[high] for t in (up3, up2, up1)]
    )
    grad_pre = (own + jnp.concatenate([low_sum, high_sum], axis=0)) * slope
    totals = []
    for g in range(GROUPS):
        totals = weight_term(act_mine[g], act_theirs[g], groups[g], totals)
    grad_w = totals[0] + swap(totals[1])
    sums = jnp.concatenate(sums, axis=0)
    sums = jnp.concatenate([sums, swap(sums)], axis=0)
    grad_bias = jnp.sum(sums[piece_of], axis=0)
    return grad_pre.T, grad_w, grad_bias


def solution(mesh):
    in_specs = (P("text", "tile"), P(), P("tile", "text"), P("text", "tile"))
    out_specs = (P("tile", "text"), P("text", "tile"), P("tile"))
    return jax.shard_map(body, mesh=mesh, in_specs=in_specs, out_specs=out_specs, check_vma=False)
```

```python
import functools

import jax
import jax.numpy as jnp
from jax import lax
from jax.experimental import pallas as pl
from jax.experimental.pallas import tpu as pltpu
from jax.sharding import PartitionSpec as P

SIDE = 4
N_TEXT = 2 * SIDE * SIDE
N_TILE = 8
ROWS = 320
HID = 160
BLOCK = 1280
SLOTS = 10240
WIDTH = 1024
LANES = 128
GROUPS = 4
GROUP_ROWS = 4 * ROWS
UNROLL = 32
HALF = HID // 2
VMEM_LIMIT = 58 * 2**20
F32 = jnp.float32
BF16 = jnp.bfloat16


def plane_perm(step0, step1):
    pairs = []
    for y in range(SIDE):
        for x in range(SIDE):
            for core, (dy, dx) in ((0, step0), (1, step1)):
                target = (((y + dy) % SIDE) * SIDE + (x + dx) % SIDE) * 2 + core
                pairs.append(((y * SIDE + x) * 2 + core, target))
    return pairs


FIRST_UP = plane_perm((0, 1), (1, 0))
FIRST_DOWN = plane_perm((0, -1), (-1, 0))
SECOND_UP = plane_perm((1, 0), (0, 1))
SECOND_DOWN = plane_perm((-1, 0), (0, -1))
SWAP = [(i, i ^ 1) for i in range(N_TEXT)]
TILE_UP = [(i, (i + 1) % N_TILE) for i in range(N_TILE)]
TILE_DOWN = [(i, (i - 1) % N_TILE) for i in range(N_TILE)]


def gather_pieces(grad):
    send = lambda value, perm: lax.ppermute(value, "text", perm)
    near, far_side = send(grad, FIRST_UP), send(grad, FIRST_DOWN)
    row = [grad, near, send(near, FIRST_UP), far_side]
    up = [send(piece, SECOND_UP) for piece in row]
    down = [send(piece, SECOND_DOWN) for piece in row]
    far = [send(up[0], SECOND_UP), send(up[1], SECOND_UP), send(down[2], SECOND_DOWN), send(down[3], SECOND_DOWN)]
    return row, up, down, far


def arrival_place(device, me):
    core, x, y = device & 1, (device >> 1) & 3, device >> 3
    my_core, my_x, my_y = me & 1, (me >> 1) & 3, me >> 3
    dx, dy = (my_x - x) & 3, (my_y - y) & 3
    first = jnp.where(core == 0, dx, dy)
    second = jnp.where(core == 0, dy, dx)
    return (core ^ my_core) * 16 + (second ^ (second >> 1)) * 4 + first


def store_rows(ref, start, value):
    count = value.shape[0]
    ref[pl.ds(start, count, stride=2), :] = value[:, :LANES]
    ref[pl.ds(start + 1, count, stride=2), 0:HID - LANES] = value[:, LANES:]


def load_turned(ref, start, count):
    left = ref[pl.ds(start, count, stride=2), :].T
    right = ref[pl.ds(start + 1, count, stride=2), :].T
    return left, right[0:HID - LANES]


def act_kernel(place_ref, act_ref, mine_ref, theirs_ref, rows, turned):
    block = pl.program_id(0)
    store_rows(turned, 0, act_ref[0].astype(F32).T)

    @pl.loop(0, BLOCK, step=UNROLL)
    def _(start):
        held = [turned[pl.ds(pl.multiple_of(2 * start, 2) + 2 * i, 2), :] for i in range(UNROLL)]
        for i in range(UNROLL):
            where = pl.multiple_of(place_ref[block * BLOCK + start + i], 2)
            rows[pl.ds(where, 2), :] = held[i]

    @pl.when(block == N_TILE - 1)
    def _():
        for group in range(2 * GROUPS):
            left, right = load_turned(rows, group * 2 * GROUP_ROWS, GROUP_ROWS)
            out_ref = (mine_ref, theirs_ref)[group // GROUPS]
            out_ref[group % GROUPS, 0:LANES, :] = left.astype(BF16)
            out_ref[group % GROUPS, LANES:HID, :] = right.astype(BF16)


def act_in_arrival_order(place, act):
    return pl.pallas_call(
        act_kernel,
        out_shape=[jax.ShapeDtypeStruct((GROUPS, HID, GROUP_ROWS), BF16)] * 2,
        grid_spec=pltpu.PrefetchScalarGridSpec(
            num_scalar_prefetch=1,
            grid=(N_TILE,),
            in_specs=[pl.BlockSpec((1, HID, BLOCK), lambda i, place: (i, 0, 0))],
            out_specs=[pl.BlockSpec((GROUPS, HID, GROUP_ROWS), lambda i, place: (0, 0, 0))] * 2,
            scratch_shapes=[pltpu.VMEM((2 * SLOTS, LANES), F32), pltpu.VMEM((2 * BLOCK, LANES), F32)],
        ),
        compiler_params=pltpu.CompilerParams(vmem_limit_bytes=VMEM_LIMIT),
        cost_estimate=pl.CostEstimate(flops=0, bytes_accessed=70_000_000, transcendentals=0),
        name="act_rows",
    )(place, act)


def product_kernel(weight_ref, *refs):
    pieces, (mine_out, theirs_out, sums_ref, mine_ref, theirs_ref, pieces_ref, sems) = refs[:4], refs[-7:]
    rows = 2 * ROWS
    copies = [pltpu.make_async_copy(pieces[k], pieces_ref.at[k], sems.at[2, k]) for k in range(4)]
    for copy in copies:
        copy.start()
    for k in range(4):
        copies.pop(0).wait()
        piece = pieces_ref[k]
        term = lax.dot_general(piece, weight_ref[...], (((1,), (1,)), ((), ())), preferred_element_type=F32)
        store_rows(mine_ref, 2 * k * ROWS, term[:, :HID])
        store_rows(theirs_ref, 2 * k * ROWS, term[:, HID:])
        for half, (held, out) in enumerate(((mine_ref, mine_out), (theirs_ref, theirs_out))):
            part = pl.ds(k * rows, rows)
            copies.append(pltpu.make_async_copy(held.at[part, :], out.at[part, :], sems.at[half, k]))
            copies[-1].start()
        sums_ref[k:k + 1, :] = jnp.sum(piece.astype(F32), axis=0, keepdims=True)
    for copy in copies:
        copy.wait()


def products_of(weight, pieces, after):
    vmem = pl.BlockSpec(memory_space=pltpu.VMEM)
    half = jax.ShapeDtypeStruct((2 * GROUP_ROWS, LANES), F32)
    return pl.pallas_call(
        product_kernel,
        out_shape=(half, half, jax.ShapeDtypeStruct((4, WIDTH), F32)),
        in_specs=[vmem] + [pl.BlockSpec(memory_space=pl.ANY)] * (4 + len(after)),
        out_specs=[pl.BlockSpec(memory_space=pl.ANY)] * 2 + [vmem],
        scratch_shapes=[
            pltpu.VMEM(half.shape, F32),
            pltpu.VMEM(half.shape, F32),
            pltpu.VMEM((4, ROWS, WIDTH), BF16),
            pltpu.SemaphoreType.DMA((3, 4)),
        ],
        compiler_params=pltpu.CompilerParams(vmem_limit_bytes=VMEM_LIMIT),
        cost_estimate=pl.CostEstimate(flops=1_300_000_000, bytes_accessed=8_000_000, transcendentals=0),
        name="products",
    )(weight, *pieces, *after)


def slot_kernel(count, place_ref, blocks_ref, *refs):
    parts, (slots_ref, out_ref, rows, picked, sems) = refs[:8], refs[-5:]
    copies = [
        pltpu.make_async_copy(part, rows.at[pl.ds(k * 2 * GROUP_ROWS, 2 * GROUP_ROWS), :], sems.at[k])
        for k, part in enumerate(parts)
    ]
    for copy in copies:
        copy.start()
    for copy in copies:
        copy.wait()

    @pl.loop(0, count)
    def _(b):
        base = blocks_ref[b] * BLOCK

        @pl.loop(0, BLOCK, step=UNROLL)
        def _(start):
            held = []
            for i in range(UNROLL):
                where = pl.multiple_of(place_ref[base + start + i], 2)
                held.append(rows[pl.ds(where, 2), :])
            for i in range(UNROLL):
                picked[pl.ds(pl.multiple_of(2 * start, 2) + 2 * i, 2), :] = held[i]

        left, right = load_turned(picked, 0, BLOCK)
        out_ref[b, 0:LANES, :] = left
        out_ref[b, LANES:HID, :] = right
        pltpu.make_async_copy(out_ref.at[b], slots_ref.at[b], sems.at[b]).start()

    for b in range(count):
        pltpu.make_async_copy(out_ref.at[b], slots_ref.at[b], sems.at[b]).wait()


def to_slot_order(place, blocks, parts, after):
    count = blocks.shape[0]
    return pl.pallas_call(
        functools.partial(slot_kernel, count),
        out_shape=jax.ShapeDtypeStruct((count, HID, BLOCK), F32),
        in_specs=[pl.BlockSpec(memory_space=pltpu.SMEM)] * 2 + [pl.BlockSpec(memory_space=pl.ANY)] * (8 + len(after)),
        out_specs=pl.BlockSpec(memory_space=pl.ANY),
        scratch_shapes=[
            pltpu.VMEM((count, HID, BLOCK), F32),
            pltpu.VMEM((2 * SLOTS, LANES), F32),
            pltpu.VMEM((2 * BLOCK, LANES), F32),
            pltpu.SemaphoreType.DMA((8,)),
        ],
        compiler_params=pltpu.CompilerParams(vmem_limit_bytes=VMEM_LIMIT),
        cost_estimate=pl.CostEstimate(flops=0, bytes_accessed=10_000_000 + 7_000_000 * count, transcendentals=0),
        name="slot_rows",
    )(place, blocks, *parts, *after)


def weight_kernel(first, mine_ref, theirs_ref, *refs):
    pieces = refs[:4]
    out_mine, out_theirs, held, sems = refs[-4:]
    copies = [
        pltpu.make_async_copy(piece, held.at[pl.ds(k * ROWS, ROWS), :], sems.at[k]) for k, piece in enumerate(pieces)
    ]
    for copy in copies:
        copy.start()
    for copy in copies:
        copy.wait()
    act = jnp.concatenate([mine_ref[...], theirs_ref[...]], axis=0)
    for n in range(0, WIDTH, 256):
        columns = slice(n, n + 256)
        term = jnp.dot(act, held[:, columns], preferred_element_type=F32)
        out_mine[:, columns] = term[:HID] if first else refs[4][:, columns] + term[:HID]
        out_theirs[:, columns] = term[HID:] if first else refs[5][:, columns] + term[HID:]


def weight_term(mine, theirs, pieces, totals):
    vmem = pl.BlockSpec(memory_space=pltpu.VMEM)
    return pl.pallas_call(
        functools.partial(weight_kernel, not totals),
        out_shape=[jax.ShapeDtypeStruct((HID, WIDTH), F32)] * 2,
        in_specs=[vmem] * 2 + [pl.BlockSpec(memory_space=pl.ANY)] * 4 + [vmem] * len(totals),
        out_specs=[vmem] * 2,
        scratch_shapes=[pltpu.VMEM((GROUP_ROWS, WIDTH), BF16), pltpu.SemaphoreType.DMA((4,))],
        compiler_params=pltpu.CompilerParams(vmem_limit_bytes=VMEM_LIMIT),
        cost_estimate=pl.CostEstimate(flops=1_300_000_000, bytes_accessed=8_000_000, transcendentals=0),
        name="weight_term",
    )(mine, theirs, *pieces, *totals)


def gelu_parts(pre):
    value = pre.astype(F32)
    cdf = 0.5 * (1.0 + jax.scipy.special.erf(value * 0.7071067811865476))
    activated = value * cdf
    slope = cdf + value * jnp.exp(-0.5 * value * value) * 0.3989422804014327
    return activated, slope


def body(grad_seq, positions, pre_act, w_out):
    me = lax.axis_index("text")
    place = 2 * (arrival_place(positions // ROWS, me) * ROWS + positions % ROWS)
    piece_of = arrival_place(jnp.arange(N_TEXT, dtype=jnp.int32), me)

    activated, slope = gelu_parts(pre_act.T)
    act_all = lax.all_gather(activated.astype(BF16), "tile", axis=0)
    swap = lambda value: lax.ppermute(value, "text", SWAP)
    groups = gather_pieces(grad_seq)
    weight = jnp.concatenate([w_out, swap(w_out)], axis=0)
    act_mine, act_theirs = act_in_arrival_order(place, act_all)
    act_theirs = swap(act_theirs)

    mine, theirs, sums = [], [], []
    for g in range(GROUPS):
        kept, sent, part = products_of(weight, groups[g], [act_mine] if g == GROUPS - 1 else [])
        mine.append(kept)
        theirs.append(swap(sent))
        sums.append(part)
    parts = mine + theirs
    tile = lax.axis_index("tile")
    early = to_slot_order(place, (tile + jnp.array([4, 3, 5], jnp.int32)) % N_TILE, parts, [])
    late = to_slot_order(place, (tile + jnp.array([2, 6, 1, 7, 0], jnp.int32)) % N_TILE, parts, [early])
    up = lambda value: lax.ppermute(value.astype(BF16), "tile", TILE_UP).astype(F32)
    down = lambda value: lax.ppermute(value.astype(BF16), "tile", TILE_DOWN).astype(F32)
    rise, fall = up(early[0, :HALF]), down(early[0, HALF:])
    rise = up(jnp.concatenate([rise + early[1, :HALF], early[1, HALF:]], axis=0))
    fall = down(jnp.concatenate([early[2, :HALF], fall + early[2, HALF:]], axis=0))
    rise, fall = up(rise + late[0]), down(fall + late[1])
    rise, fall = up(rise + late[2]), down(fall + late[3])
    grad_pre = (late[4] + rise + fall) * slope
    totals = []
    for g in range(GROUPS):
        totals = weight_term(act_mine[g], act_theirs[g], groups[g], totals)
    grad_w = totals[0] + swap(totals[1])
    sums = jnp.concatenate(sums, axis=0)
    sums = jnp.concatenate([sums, swap(sums)], axis=0)
    grad_bias = jnp.sum(sums[piece_of], axis=0)
    return grad_pre.T, grad_w, grad_bias


def solution(mesh):
    in_specs = (P("text", "tile"), P(), P("tile", "text"), P("text", "tile"))
    out_specs = (P("tile", "text"), P("text", "tile"), P("tile"))
    return jax.shard_map(body, mesh=mesh, in_specs=in_specs, out_specs=out_specs, check_vma=False)
```

```python
import functools

import jax
import jax.numpy as jnp
from jax import lax
from jax.experimental import pallas as pl
from jax.experimental.pallas import tpu as pltpu
from jax.sharding import PartitionSpec as P

SIDE = 4
N_TEXT = 2 * SIDE * SIDE
N_TILE = 8
ROWS = 320
HID = 160
BLOCK = 1280
SLOTS = 10240
WIDTH = 1024
HALF = HID // 2
LANES = 128
GROUPS = 4
GROUP_ROWS = 4 * ROWS
UNROLL = 32
F32 = jnp.float32
BF16 = jnp.bfloat16


def plane_perm(step0, step1):
    pairs = []
    for y in range(SIDE):
        for x in range(SIDE):
            for core, (dy, dx) in ((0, step0), (1, step1)):
                target = (((y + dy) % SIDE) * SIDE + (x + dx) % SIDE) * 2 + core
                pairs.append(((y * SIDE + x) * 2 + core, target))
    return pairs


FIRST_UP = plane_perm((0, 1), (1, 0))
FIRST_DOWN = plane_perm((0, -1), (-1, 0))
SECOND_UP = plane_perm((1, 0), (0, 1))
SECOND_DOWN = plane_perm((-1, 0), (0, -1))
ARRIVAL = [(0, 0), (1, 0), (3, 0), (0, 1), (0, 3), (1, 1), (2, 0), (3, 1), (1, 3), (3, 3), (0, 2), (2, 1), (2, 3), (1, 2), (3, 2), (2, 2)]
SWAP = [(i, i ^ 1) for i in range(N_TEXT)]
TILE_UP = [(i, (i + 1) % N_TILE) for i in range(N_TILE)]
TILE_DOWN = [(i, (i - 1) % N_TILE) for i in range(N_TILE)]


def arrival_place(device, me):
    core, x, y = device & 1, (device >> 1) & 3, device >> 3
    my_core, my_x, my_y = me & 1, (me >> 1) & 3, me >> 3
    dx, dy = (my_x - x) & 3, (my_y - y) & 3
    first = jnp.where(core == 0, dx, dy)
    second = jnp.where(core == 0, dy, dx)
    codes = [sum(ARRIVAL.index((i, j)) << (4 * i) for i in range(SIDE)) for j in range(SIDE)]
    code = jnp.where(second == 0, codes[0], jnp.where(second == 1, codes[1], jnp.where(second == 2, codes[2], codes[3])))
    return (core ^ my_core) * 16 + ((code >> (4 * first)) & 15)


def store_rows(ref, start, value):
    count = value.shape[0]
    ref[pl.ds(start, count, stride=2), :] = value[:, :LANES]
    ref[pl.ds(start + 1, count, stride=2), 0:HID - LANES] = value[:, LANES:]


def load_turned(ref, start, count):
    left = ref[pl.ds(start, count, stride=2), :].T
    right = ref[pl.ds(start + 1, count, stride=2), :].T
    return left, right[0:HID - LANES]


def act_kernel(place_ref, act_ref, mine_ref, theirs_ref, rows, turned):
    block = pl.program_id(0)
    store_rows(turned, 0, act_ref[0].astype(F32).T)

    @pl.loop(0, BLOCK, step=UNROLL)
    def _(start):
        held = [turned[pl.ds(pl.multiple_of(2 * start, 2) + 2 * i, 2), :] for i in range(UNROLL)]
        for i in range(UNROLL):
            where = pl.multiple_of(place_ref[block * BLOCK + start + i], 2)
            rows[pl.ds(where, 2), :] = held[i]

    @pl.when(block == N_TILE - 1)
    def _():
        for group in range(2 * GROUPS):
            left, right = load_turned(rows, group * 2 * GROUP_ROWS, GROUP_ROWS)
            out_ref = (mine_ref, theirs_ref)[group // GROUPS]
            out_ref[group % GROUPS, 0:LANES, :] = left.astype(BF16)
            out_ref[group % GROUPS, LANES:HID, :] = right.astype(BF16)


def act_in_arrival_order(place, act):
    return pl.pallas_call(
        act_kernel,
        out_shape=[jax.ShapeDtypeStruct((GROUPS, HID, GROUP_ROWS), BF16)] * 2,
        grid_spec=pltpu.PrefetchScalarGridSpec(
            num_scalar_prefetch=1,
            grid=(N_TILE,),
            in_specs=[pl.BlockSpec((1, HID, BLOCK), lambda i, place: (i, 0, 0))],
            out_specs=[pl.BlockSpec((GROUPS, HID, GROUP_ROWS), lambda i, place: (0, 0, 0), pipeline_mode=pl.Buffered(1))] * 2,
            scratch_shapes=[pltpu.VMEM((2 * SLOTS, LANES), F32), pltpu.VMEM((2 * BLOCK, LANES), F32)],
        ),
        compiler_params=pltpu.CompilerParams(vmem_limit_bytes=17 * 2**20),
        cost_estimate=pl.CostEstimate(flops=0, bytes_accessed=70_000_000, transcendentals=0),
        name="act_rows",
    )(place, act)


def product_kernel(hand_on, weight_ref, *refs):
    pieces = refs[:4]
    if hand_on is None:
        mine_ref, theirs_ref, sums_ref = refs[-3:]
    else:
        mine_ref, theirs_ref, sums_ref, next_ref, sem = refs[-5:]
        copy = pltpu.make_async_copy(pieces[hand_on], next_ref, sem)
        copy.start()
    for k in range(4):
        piece = pieces[k][...]
        term = lax.dot_general(piece, weight_ref[...], (((1,), (1,)), ((), ())), preferred_element_type=F32)
        store_rows(mine_ref, 2 * k * ROWS, term[:, :HID])
        store_rows(theirs_ref, 2 * k * ROWS, term[:, HID:])
        sums_ref[k:k + 1, :] = jnp.sum(piece.astype(F32), axis=0, keepdims=True)
    if hand_on is not None:
        copy.wait()


def products_of(weight, pieces, after, hand_on=None):
    vmem, anywhere = pl.BlockSpec(memory_space=pltpu.VMEM), pl.BlockSpec(memory_space=pl.ANY)
    half = jax.ShapeDtypeStruct((2 * GROUP_ROWS, LANES), F32)
    out = [pltpu.VMEM(half.shape, F32), half, jax.ShapeDtypeStruct((4, WIDTH), F32)]
    return pl.pallas_call(
        functools.partial(product_kernel, hand_on),
        out_shape=out + [jax.ShapeDtypeStruct((ROWS, WIDTH), BF16)] * (hand_on is not None),
        in_specs=[vmem] * 5 + [anywhere] * len(after),
        out_specs=[vmem] * 3 + [anywhere] * (hand_on is not None),
        scratch_shapes=[pltpu.SemaphoreType.DMA(())] * (hand_on is not None),
        compiler_params=pltpu.CompilerParams(vmem_limit_bytes=6 * 2**20),
        cost_estimate=pl.CostEstimate(flops=1_300_000_000, bytes_accessed=8_000_000, transcendentals=0),
        name="products",
    )(weight, *pieces, *after)


def slot_kernel(count, place_ref, blocks_ref, *refs):
    if len(refs) == 3:
        rows_ref, out_ref, picked = refs
    else:
        rows_ref, out_ref, picked, sems = refs[8:]
        copies = [
            pltpu.make_async_copy(refs[k], rows_ref.at[pl.ds(k * 2 * GROUP_ROWS, 2 * GROUP_ROWS), :], sems.at[k])
            for k in range(8)
        ]
        for copy in copies:
            copy.start()
        for copy in copies:
            copy.wait()

    @pl.loop(0, count)
    def _(b):
        base = blocks_ref[b] * BLOCK

        @pl.loop(0, BLOCK, step=UNROLL)
        def _(start):
            held = []
            for i in range(UNROLL):
                where = pl.multiple_of(place_ref[base + start + i], 2)
                held.append(rows_ref[pl.ds(where, 2), :])
            for i in range(UNROLL):
                picked[pl.ds(pl.multiple_of(2 * start, 2) + 2 * i, 2), :] = held[i]

        left, right = load_turned(picked, 0, BLOCK)
        out_ref[b, 0:LANES, :] = left
        out_ref[b, LANES:HID, :] = right


def to_slot_order(place, blocks, rows):
    count = blocks.shape[0]
    vmem = pl.BlockSpec(memory_space=pltpu.VMEM)
    out = [pltpu.VMEM((count, HID, BLOCK), F32)]
    whole = len(rows) == 1
    if not whole:
        out.insert(0, pltpu.VMEM((2 * SLOTS, LANES), F32))
    return pl.pallas_call(
        functools.partial(slot_kernel, count),
        out_shape=out,
        in_specs=[pl.BlockSpec(memory_space=pltpu.SMEM)] * 2
        + ([vmem] if whole else [pl.BlockSpec(memory_space=pl.ANY)] * len(rows)),
        out_specs=[vmem] * len(out),
        scratch_shapes=[pltpu.VMEM((2 * BLOCK, LANES), F32)] + [pltpu.SemaphoreType.DMA((8,))] * (not whole),
        compiler_params=pltpu.CompilerParams(vmem_limit_bytes=(5 if whole else 46) * 2**20),
        cost_estimate=pl.CostEstimate(flops=0, bytes_accessed=8_000_000 * count, transcendentals=0),
        name="slot_rows",
    )(place, blocks, *rows)


def weight_kernel(first, mine_ref, theirs_ref, *refs):
    pieces = refs[:4]
    out_mine, out_theirs, held, sems = refs[-4:]
    copies = [
        pltpu.make_async_copy(piece, held.at[pl.ds(k * ROWS, ROWS), :], sems.at[k]) for k, piece in enumerate(pieces)
    ]
    for copy in copies:
        copy.start()
    for copy in copies:
        copy.wait()
    act = jnp.concatenate([mine_ref[...], theirs_ref[...]], axis=0)
    for n in range(0, WIDTH, 256):
        columns = slice(n, n + 256)
        term = jnp.dot(act, held[:, columns], preferred_element_type=F32)
        out_mine[:, columns] = term[:HID] if first else refs[4][:, columns] + term[:HID]
        out_theirs[:, columns] = term[HID:] if first else refs[5][:, columns] + term[HID:]


def weight_term(mine, theirs, pieces, totals):
    vmem = pl.BlockSpec(memory_space=pltpu.VMEM)
    return pl.pallas_call(
        functools.partial(weight_kernel, not totals),
        out_shape=[jax.ShapeDtypeStruct((HID, WIDTH), F32)] * 2,
        in_specs=[vmem] * 2 + [pl.BlockSpec(memory_space=pl.ANY)] * 4 + [vmem] * len(totals),
        out_specs=[vmem] * 2,
        scratch_shapes=[pltpu.VMEM((GROUP_ROWS, WIDTH), BF16), pltpu.SemaphoreType.DMA((4,))],
        compiler_params=pltpu.CompilerParams(vmem_limit_bytes=6 * 2**20),
        cost_estimate=pl.CostEstimate(flops=1_300_000_000, bytes_accessed=8_000_000, transcendentals=0),
        name="weight_term",
    )(mine, theirs, *pieces, *totals)


def gelu_parts(pre):
    value = pre.astype(F32)
    cdf = 0.5 * (1.0 + jax.scipy.special.erf(value * 0.7071067811865476))
    activated = value * cdf
    slope = cdf + value * jnp.exp(-0.5 * value * value) * 0.3989422804014327
    return activated, slope


def body(grad_seq, positions, pre_act, w_out):
    me = lax.axis_index("text")
    place = 2 * (arrival_place(positions // ROWS, me) * ROWS + positions % ROWS)
    piece_of = arrival_place(jnp.arange(N_TEXT, dtype=jnp.int32), me)

    activated, slope = gelu_parts(pre_act.T)
    act_all = lax.all_gather(activated.astype(BF16), "tile", axis=0)
    swap = lambda value: lax.ppermute(value, "text", SWAP)
    send = lambda value, perm: lax.ppermute(value, "text", perm)
    weight = jnp.concatenate([w_out, swap(w_out)], axis=0)
    act_mine, act_theirs = act_in_arrival_order(place, act_all)
    act_theirs = swap(act_theirs)

    got = {(0, 0): grad_seq, (1, 0): send(grad_seq, FIRST_UP), (3, 0): send(grad_seq, FIRST_DOWN)}
    got[0, 1], got[0, 3] = send(grad_seq, SECOND_UP), send(grad_seq, SECOND_DOWN)
    got[2, 0] = send(got[1, 0], FIRST_UP)
    for first in (1, 3, 2):
        got[first, 1], got[first, 3] = send(got[first, 0], SECOND_UP), send(got[first, 0], SECOND_DOWN)
    mine, theirs, sums = [], [], []
    for g in range(GROUPS):
        pieces = [got[key] for key in ARRIVAL[4 * g:4 * g + 4]]
        after = [act_mine] if g == GROUPS - 1 else []
        kept, sent, part, *handed = products_of(weight, pieces, after, {0: 3, 1: 1}.get(g))
        if g == 0:
            got[0, 2] = send(handed[0], SECOND_UP)
        if g == 1:
            got[1, 2] = send(handed[0], SECOND_UP)
            got[3, 2], got[2, 2] = send(got[3, 3], SECOND_DOWN), send(got[2, 3], SECOND_DOWN)
        mine.append(kept)
        theirs.append(swap(sent))
        sums.append(part)
    groups = [[got[key] for key in ARRIVAL[4 * g:4 * g + 4]] for g in range(GROUPS)]
    tile = lax.axis_index("tile")
    rows, early = to_slot_order(place, (tile + jnp.array([4, 3, 5], jnp.int32)) % N_TILE, mine + theirs)
    (late,) = to_slot_order(place, (tile + jnp.array([2, 6, 1, 7, 0], jnp.int32)) % N_TILE, [rows])
    up = lambda value: lax.ppermute(value.astype(BF16), "tile", TILE_UP).astype(F32)
    down = lambda value: lax.ppermute(value.astype(BF16), "tile", TILE_DOWN).astype(F32)
    rise, fall = up(early[0, :HALF]), down(early[0, HALF:])
    rise = up(jnp.concatenate([rise + early[1, :HALF], early[1, HALF:]], axis=0))
    fall = down(jnp.concatenate([early[2, :HALF], fall + early[2, HALF:]], axis=0))
    rise, fall = up(rise + late[0]), down(fall + late[1])
    rise, fall = up(rise + late[2]), down(fall + late[3])
    grad_pre = (late[4] + rise + fall) * slope
    totals = []
    for g in range(GROUPS):
        totals = weight_term(act_mine[g], act_theirs[g], groups[g], totals)
    grad_w = totals[0] + swap(totals[1])
    sums = jnp.concatenate(sums, axis=0)
    sums = jnp.concatenate([sums, swap(sums)], axis=0)
    grad_bias = jnp.sum(sums[piece_of], axis=0)
    return grad_pre.T, grad_w, grad_bias


def solution(mesh):
    in_specs = (P("text", "tile"), P(), P("tile", "text"), P("text", "tile"))
    out_specs = (P("tile", "text"), P("text", "tile"), P("tile"))
    return jax.shard_map(body, mesh=mesh, in_specs=in_specs, out_specs=out_specs, check_vma=False)
```

```python
import functools

import jax
import jax.numpy as jnp
from jax import lax
from jax.experimental import pallas as pl
from jax.experimental.pallas import tpu as pltpu
from jax.sharding import PartitionSpec as P

SIDE = 4
N_TEXT = 2 * SIDE * SIDE
N_TILE = 8
ROWS = 320
HID = 160
BLOCK = 1280
SLOTS = 10240
WIDTH = 1024
HALF = HID // 2
LANES = 128
GROUPS = 4
GROUP_ROWS = 4 * ROWS
UNROLL = 32
F32 = jnp.float32
BF16 = jnp.bfloat16


def plane_perm(step0, step1):
    pairs = []
    for y in range(SIDE):
        for x in range(SIDE):
            for core, (dy, dx) in ((0, step0), (1, step1)):
                target = (((y + dy) % SIDE) * SIDE + (x + dx) % SIDE) * 2 + core
                pairs.append(((y * SIDE + x) * 2 + core, target))
    return pairs


FIRST_UP = plane_perm((0, 1), (1, 0))
FIRST_DOWN = plane_perm((0, -1), (-1, 0))
SECOND_UP = plane_perm((1, 0), (0, 1))
SECOND_DOWN = plane_perm((-1, 0), (0, -1))
ARRIVAL = [(0, 0), (1, 0), (3, 0), (0, 1), (0, 3), (1, 1), (2, 0), (3, 1), (1, 3), (3, 3), (0, 2), (2, 1), (2, 3), (1, 2), (3, 2), (2, 2)]
SWAP = [(i, i ^ 1) for i in range(N_TEXT)]
TILE_UP = [(i, (i + 1) % N_TILE) for i in range(N_TILE)]
TILE_DOWN = [(i, (i - 1) % N_TILE) for i in range(N_TILE)]


def arrival_place(device, me):
    core, x, y = device & 1, (device >> 1) & 3, device >> 3
    my_core, my_x, my_y = me & 1, (me >> 1) & 3, me >> 3
    dx, dy = (my_x - x) & 3, (my_y - y) & 3
    first = jnp.where(core == 0, dx, dy)
    second = jnp.where(core == 0, dy, dx)
    codes = [sum(ARRIVAL.index((i, j)) << (4 * i) for i in range(SIDE)) for j in range(SIDE)]
    code = jnp.where(second == 0, codes[0], jnp.where(second == 1, codes[1], jnp.where(second == 2, codes[2], codes[3])))
    return (core ^ my_core) * 16 + ((code >> (4 * first)) & 15)


def store_rows(ref, start, value):
    count = value.shape[0]
    ref[pl.ds(start, count, stride=2), :] = value[:, :LANES]
    ref[pl.ds(start + 1, count, stride=2), 0:HID - LANES] = value[:, LANES:]


def load_turned(ref, start, count):
    left = ref[pl.ds(start, count, stride=2), :].T
    right = ref[pl.ds(start + 1, count, stride=2), :].T
    return left, right[0:HID - LANES]


def act_kernel(place_ref, act_ref, mine_ref, theirs_ref, rows, turned):
    block = pl.program_id(0)
    store_rows(turned, 0, act_ref[0].astype(F32).T)

    @pl.loop(0, BLOCK, step=UNROLL)
    def _(start):
        held = [turned[pl.ds(pl.multiple_of(2 * start, 2) + 2 * i, 2), :] for i in range(UNROLL)]
        for i in range(UNROLL):
            where = pl.multiple_of(place_ref[block * BLOCK + start + i], 2)
            rows[pl.ds(where, 2), :] = held[i]

    @pl.when(block == N_TILE - 1)
    def _():
        for group in range(2 * GROUPS):
            left, right = load_turned(rows, group * 2 * GROUP_ROWS, GROUP_ROWS)
            out_ref = (mine_ref, theirs_ref)[group // GROUPS]
            out_ref[group % GROUPS, 0:LANES, :] = left.astype(BF16)
            out_ref[group % GROUPS, LANES:HID, :] = right.astype(BF16)


def act_in_arrival_order(place, act):
    return pl.pallas_call(
        act_kernel,
        out_shape=[jax.ShapeDtypeStruct((GROUPS, HID, GROUP_ROWS), BF16)] * 2,
        grid_spec=pltpu.PrefetchScalarGridSpec(
            num_scalar_prefetch=1,
            grid=(N_TILE,),
            in_specs=[pl.BlockSpec((1, HID, BLOCK), lambda i, place: (i, 0, 0))],
            out_specs=[pl.BlockSpec((GROUPS, HID, GROUP_ROWS), lambda i, place: (0, 0, 0), pipeline_mode=pl.Buffered(1))] * 2,
            scratch_shapes=[pltpu.VMEM((2 * SLOTS, LANES), F32), pltpu.VMEM((2 * BLOCK, LANES), F32)],
        ),
        compiler_params=pltpu.CompilerParams(vmem_limit_bytes=17 * 2**20),
        cost_estimate=pl.CostEstimate(flops=0, bytes_accessed=70_000_000, transcendentals=0),
        name="act_rows",
    )(place, act)


def product_kernel(hand_on, weight_ref, *refs):
    pieces = refs[:4]
    if hand_on is None:
        mine_ref, theirs_ref, sums_ref = refs[-3:]
    else:
        mine_ref, theirs_ref, sums_ref, next_ref, sem = refs[-5:]
        copy = pltpu.make_async_copy(pieces[hand_on], next_ref, sem)
        copy.start()
    for k in range(4):
        piece = pieces[k][...]
        term = lax.dot_general(piece, weight_ref[...], (((1,), (1,)), ((), ())), preferred_element_type=F32)
        store_rows(mine_ref, 2 * k * ROWS, term[:, :HID])
        store_rows(theirs_ref, 2 * k * ROWS, term[:, HID:])
        sums_ref[k:k + 1, :] = jnp.sum(piece.astype(F32), axis=0, keepdims=True)
    if hand_on is not None:
        copy.wait()


def products_of(weight, pieces, after, hand_on=None):
    vmem, anywhere = pl.BlockSpec(memory_space=pltpu.VMEM), pl.BlockSpec(memory_space=pl.ANY)
    half = jax.ShapeDtypeStruct((2 * GROUP_ROWS, LANES), F32)
    out = [pltpu.VMEM(half.shape, F32), half, jax.ShapeDtypeStruct((4, WIDTH), F32)]
    return pl.pallas_call(
        functools.partial(product_kernel, hand_on),
        out_shape=out + [jax.ShapeDtypeStruct((ROWS, WIDTH), BF16)] * (hand_on is not None),
        in_specs=[vmem] * 5 + [anywhere] * len(after),
        out_specs=[vmem] * 3 + [anywhere] * (hand_on is not None),
        scratch_shapes=[pltpu.SemaphoreType.DMA(())] * (hand_on is not None),
        compiler_params=pltpu.CompilerParams(vmem_limit_bytes=6 * 2**20),
        cost_estimate=pl.CostEstimate(flops=1_300_000_000, bytes_accessed=8_000_000, transcendentals=0),
        name="products",
    )(weight, *pieces, *after)


def slot_kernel(count, gather_rows, keep, place_ref, blocks_ref, *refs):
    if gather_rows:
        rows_ref, out_ref, picked, sems = refs[-4:] if keep else (refs[-1], *refs[-4:-1])
        copies = [
            pltpu.make_async_copy(refs[k], rows_ref.at[pl.ds(k * 2 * GROUP_ROWS, 2 * GROUP_ROWS), :], sems.at[k])
            for k in range(8)
        ]
        for copy in copies:
            copy.start()
        for copy in copies:
            copy.wait()
    else:
        rows_ref, (out_ref, picked) = refs[0], refs[-2:]

    @pl.loop(0, count)
    def _(b):
        base = blocks_ref[b] * BLOCK

        @pl.loop(0, BLOCK, step=UNROLL)
        def _(start):
            held = []
            for i in range(UNROLL):
                where = pl.multiple_of(place_ref[base + start + i], 2)
                held.append(rows_ref[pl.ds(where, 2), :])
            for i in range(UNROLL):
                picked[pl.ds(pl.multiple_of(2 * start, 2) + 2 * i, 2), :] = held[i]

        left, right = load_turned(picked, 0, BLOCK)
        out_ref[b, 0:LANES, :] = left
        out_ref[b, LANES:HID, :] = right


def to_slot_order(place, blocks, rows, after, keep=False):
    count = blocks.shape[0]
    vmem, anywhere = pl.BlockSpec(memory_space=pltpu.VMEM), pl.BlockSpec(memory_space=pl.ANY)
    out = [pltpu.VMEM((count, HID, BLOCK), F32)]
    whole = len(rows) == 1
    scratch = [pltpu.VMEM((2 * BLOCK, LANES), F32)] + [pltpu.SemaphoreType.DMA((8,))] * (not whole)
    if keep:
        out.insert(0, pltpu.VMEM((2 * SLOTS, LANES), F32))
    elif not whole:
        scratch.append(pltpu.VMEM((2 * SLOTS, LANES), F32))
    return pl.pallas_call(
        functools.partial(slot_kernel, count, not whole, keep),
        out_shape=out,
        in_specs=[pl.BlockSpec(memory_space=pltpu.SMEM)] * 2
        + [vmem if whole else anywhere] * len(rows)
        + [anywhere] * len(after),
        out_specs=[vmem] * len(out),
        scratch_shapes=scratch,
        compiler_params=pltpu.CompilerParams(vmem_limit_bytes=(5 if whole else 46) * 2**20),
        cost_estimate=pl.CostEstimate(flops=0, bytes_accessed=8_000_000 * count, transcendentals=0),
        name="slot_rows",
    )(place, blocks, *rows, *after)


def weight_kernel(first, mine_ref, theirs_ref, *refs):
    pieces = refs[:4]
    out_mine, out_theirs, held, sems = refs[-4:]
    copies = [
        pltpu.make_async_copy(piece, held.at[pl.ds(k * ROWS, ROWS), :], sems.at[k]) for k, piece in enumerate(pieces)
    ]
    for copy in copies:
        copy.start()
    for copy in copies:
        copy.wait()
    act = jnp.concatenate([mine_ref[...], theirs_ref[...]], axis=0)
    for n in range(0, WIDTH, 256):
        columns = slice(n, n + 256)
        term = jnp.dot(act, held[:, columns], preferred_element_type=F32)
        out_mine[:, columns] = term[:HID] if first else refs[4][:, columns] + term[:HID]
        out_theirs[:, columns] = term[HID:] if first else refs[5][:, columns] + term[HID:]


def weight_term(mine, theirs, pieces, totals, after):
    vmem = pl.BlockSpec(memory_space=pltpu.VMEM)
    return pl.pallas_call(
        functools.partial(weight_kernel, not totals),
        out_shape=[jax.ShapeDtypeStruct((HID, WIDTH), F32)] * 2,
        in_specs=[vmem] * 2 + [pl.BlockSpec(memory_space=pl.ANY)] * 4 + [vmem] * len(totals)
        + [pl.BlockSpec(memory_space=pl.ANY)] * len(after),
        out_specs=[vmem] * 2,
        scratch_shapes=[pltpu.VMEM((GROUP_ROWS, WIDTH), BF16), pltpu.SemaphoreType.DMA((4,))],
        compiler_params=pltpu.CompilerParams(vmem_limit_bytes=6 * 2**20),
        cost_estimate=pl.CostEstimate(flops=1_300_000_000, bytes_accessed=8_000_000, transcendentals=0),
        name="weight_term",
    )(mine, theirs, *pieces, *totals, *after)


def gelu_parts(pre):
    value = pre.astype(F32)
    cdf = 0.5 * (1.0 + jax.scipy.special.erf(value * 0.7071067811865476))
    activated = value * cdf
    slope = cdf + value * jnp.exp(-0.5 * value * value) * 0.3989422804014327
    return activated, slope


def body(grad_seq, positions, pre_act, w_out):
    me = lax.axis_index("text")
    place = 2 * (arrival_place(positions // ROWS, me) * ROWS + positions % ROWS)
    piece_of = arrival_place(jnp.arange(N_TEXT, dtype=jnp.int32), me)

    activated, slope = gelu_parts(pre_act.T)
    act_all = lax.all_gather(activated.astype(BF16), "tile", axis=0)
    swap = lambda value: lax.ppermute(value, "text", SWAP)
    send = lambda value, perm: lax.ppermute(value, "text", perm)
    weight = jnp.concatenate([w_out, swap(w_out)], axis=0)
    act_mine, act_theirs = act_in_arrival_order(place, act_all)
    act_theirs = swap(act_theirs)

    got = {(0, 0): grad_seq, (1, 0): send(grad_seq, FIRST_UP), (3, 0): send(grad_seq, FIRST_DOWN)}
    got[0, 1], got[0, 3] = send(grad_seq, SECOND_UP), send(grad_seq, SECOND_DOWN)
    got[2, 0] = send(got[1, 0], FIRST_UP)
    for first in (1, 3, 2):
        got[first, 1], got[first, 3] = send(got[first, 0], SECOND_UP), send(got[first, 0], SECOND_DOWN)
    mine, theirs, sums = [], [], []
    for g in range(GROUPS):
        pieces = [got[key] for key in ARRIVAL[4 * g:4 * g + 4]]
        after = [act_mine] if g == GROUPS - 1 else []
        kept, sent, part, *handed = products_of(weight, pieces, after, {0: 3, 1: 1}.get(g))
        if g == 0:
            got[0, 2] = send(handed[0], SECOND_UP)
        if g == 1:
            got[1, 2] = send(handed[0], SECOND_UP)
            got[3, 2], got[2, 2] = send(got[3, 3], SECOND_DOWN), send(got[2, 3], SECOND_DOWN)
        mine.append(kept)
        theirs.append(swap(sent))
        sums.append(part)
    groups = [[got[key] for key in ARRIVAL[4 * g:4 * g + 4]] for g in range(GROUPS)]
    tile = lax.axis_index("tile")
    parts = mine + theirs

    def slots(steps, rows, after, keep=False):
        return to_slot_order(place, (tile + jnp.array(steps, jnp.int32)) % N_TILE, rows, after, keep)

    rows, across = slots([4], parts, [], keep=True)
    (third,) = slots([3, 5], [rows], [across])
    up = lambda value: lax.ppermute(value.astype(BF16), "tile", TILE_UP)
    down = lambda value: lax.ppermute(value.astype(BF16), "tile", TILE_DOWN)
    rise, fall = up(across[0, :HALF]), down(across[0, HALF:])
    (second,) = slots([2, 6], parts, [rise])
    up3 = jnp.concatenate([rise.astype(F32) + third[0, :HALF], third[0, HALF:]], axis=0)
    down3 = jnp.concatenate([third[1, :HALF], fall.astype(F32) + third[1, HALF:]], axis=0)
    rise, fall = up(up3), down(down3)
    (nearest,) = slots([1, 7, 0], parts, [rise])
    rise, fall = up(rise.astype(F32) + second[0]), down(fall.astype(F32) + second[1])
    hop = rise
    rise, fall = up(rise.astype(F32) + nearest[0]), down(fall.astype(F32) + nearest[1])
    grad_pre = (nearest[2] + rise.astype(F32) + fall.astype(F32)) * lax.optimization_barrier(slope)
    totals = []
    for g in range(GROUPS):
        totals = weight_term(act_mine[g], act_theirs[g], groups[g], totals, [hop] if g == 1 else [])
    grad_w = totals[0] + swap(totals[1])
    sums = jnp.concatenate(sums, axis=0)
    sums = jnp.concatenate([sums, swap(sums)], axis=0)
    grad_bias = jnp.sum(sums[piece_of], axis=0)
    return grad_pre.T, grad_w, grad_bias


def solution(mesh):
    in_specs = (P("text", "tile"), P(), P("tile", "text"), P("text", "tile"))
    out_specs = (P("tile", "text"), P("text", "tile"), P("tile"))
    return jax.shard_map(body, mesh=mesh, in_specs=in_specs, out_specs=out_specs, check_vma=False)
```

```python
import functools

import jax
import jax.numpy as jnp
from jax import lax
from jax.experimental import pallas as pl
from jax.experimental.pallas import tpu as pltpu
from jax.sharding import PartitionSpec as P

SIDE = 4
N_TEXT = 2 * SIDE * SIDE
N_TILE = 8
ROWS = 320
HID = 160
BLOCK = 1280
SLOTS = 10240
WIDTH = 1024
HALF = HID // 2
LANES = 128
GROUPS = 4
GROUP_ROWS = 4 * ROWS
UNROLL = 32
F32 = jnp.float32
BF16 = jnp.bfloat16


def plane_perm(step0, step1):
    pairs = []
    for y in range(SIDE):
        for x in range(SIDE):
            for core, (dy, dx) in ((0, step0), (1, step1)):
                target = (((y + dy) % SIDE) * SIDE + (x + dx) % SIDE) * 2 + core
                pairs.append(((y * SIDE + x) * 2 + core, target))
    return pairs


FIRST_UP = plane_perm((0, 1), (1, 0))
FIRST_DOWN = plane_perm((0, -1), (-1, 0))
SECOND_UP = plane_perm((1, 0), (0, 1))
SECOND_DOWN = plane_perm((-1, 0), (0, -1))
ARRIVAL = [(0, 0), (1, 0), (3, 0), (0, 1), (0, 3), (1, 1), (2, 0), (3, 1), (1, 3), (3, 3), (0, 2), (2, 1), (2, 3), (1, 2), (3, 2), (2, 2)]
SWAP = [(i, i ^ 1) for i in range(N_TEXT)]
TILE_UP = [(i, (i + 1) % N_TILE) for i in range(N_TILE)]
TILE_DOWN = [(i, (i - 1) % N_TILE) for i in range(N_TILE)]


def arrival_place(device, me):
    core, x, y = device & 1, (device >> 1) & 3, device >> 3
    my_core, my_x, my_y = me & 1, (me >> 1) & 3, me >> 3
    dx, dy = (my_x - x) & 3, (my_y - y) & 3
    first = jnp.where(core == 0, dx, dy)
    second = jnp.where(core == 0, dy, dx)
    codes = [sum(ARRIVAL.index((i, j)) << (4 * i) for i in range(SIDE)) for j in range(SIDE)]
    code = jnp.where(second == 0, codes[0], jnp.where(second == 1, codes[1], jnp.where(second == 2, codes[2], codes[3])))
    return (core ^ my_core) * 16 + ((code >> (4 * first)) & 15)


def store_rows(ref, start, value):
    count = value.shape[0]
    ref[pl.ds(start, count, stride=2), :] = value[:, :LANES]
    ref[pl.ds(start + 1, count, stride=2), 0:HID - LANES] = value[:, LANES:]


def load_turned(ref, start, count):
    left = ref[pl.ds(start, count, stride=2), :].T
    right = ref[pl.ds(start + 1, count, stride=2), :].T
    return left, right[0:HID - LANES]


def act_kernel(place_ref, act_ref, piece_ref, mine_ref, theirs_ref, next_ref, rows, turned, sem):
    block = pl.program_id(0)
    copy = pltpu.make_async_copy(piece_ref, next_ref, sem)

    @pl.when(block == 0)
    def _():
        copy.start()

    store_rows(turned, 0, act_ref[0].astype(F32).T)

    @pl.loop(0, BLOCK, step=UNROLL)
    def _(start):
        held = [turned[pl.ds(pl.multiple_of(2 * start, 2) + 2 * i, 2), :] for i in range(UNROLL)]
        for i in range(UNROLL):
            where = pl.multiple_of(place_ref[block * BLOCK + start + i], 2)
            rows[pl.ds(where, 2), :] = held[i]

    @pl.when(block == N_TILE - 1)
    def _():
        for group in range(2 * GROUPS):
            left, right = load_turned(rows, group * 2 * GROUP_ROWS, GROUP_ROWS)
            out_ref = (mine_ref, theirs_ref)[group // GROUPS]
            out_ref[group % GROUPS, 0:LANES, :] = left.astype(BF16)
            out_ref[group % GROUPS, LANES:HID, :] = right.astype(BF16)
        copy.wait()


def act_in_arrival_order(place, act, piece):
    return pl.pallas_call(
        act_kernel,
        out_shape=[jax.ShapeDtypeStruct((GROUPS, HID, GROUP_ROWS), BF16)] * 2
        + [jax.ShapeDtypeStruct(piece.shape, piece.dtype)],
        grid_spec=pltpu.PrefetchScalarGridSpec(
            num_scalar_prefetch=1,
            grid=(N_TILE,),
            in_specs=[
                pl.BlockSpec((1, HID, BLOCK), lambda i, place: (i, 0, 0)),
                pl.BlockSpec(memory_space=pl.ANY),
            ],
            out_specs=[pl.BlockSpec((GROUPS, HID, GROUP_ROWS), lambda i, place: (0, 0, 0), pipeline_mode=pl.Buffered(1))] * 2
            + [pl.BlockSpec(memory_space=pl.ANY)],
            scratch_shapes=[
                pltpu.VMEM((2 * SLOTS, LANES), F32),
                pltpu.VMEM((2 * BLOCK, LANES), F32),
                pltpu.SemaphoreType.DMA(()),
            ],
        ),
        compiler_params=pltpu.CompilerParams(vmem_limit_bytes=17 * 2**20),
        cost_estimate=pl.CostEstimate(flops=0, bytes_accessed=70_000_000, transcendentals=0),
        name="act_rows",
    )(place, act, piece)


def product_kernel(hand_on, weight_ref, *refs):
    pieces = refs[:4]
    if hand_on is None:
        mine_ref, theirs_ref, sums_ref = refs[-3:]
    else:
        mine_ref, theirs_ref, sums_ref, next_ref, sem = refs[-5:]
        copy = pltpu.make_async_copy(pieces[hand_on], next_ref, sem)
        copy.start()
    for k in range(4):
        piece = pieces[k][...]
        term = lax.dot_general(piece, weight_ref[...], (((1,), (1,)), ((), ())), preferred_element_type=F32)
        store_rows(mine_ref, 2 * k * ROWS, term[:, :HID])
        store_rows(theirs_ref, 2 * k * ROWS, term[:, HID:])
        sums_ref[k:k + 1, :] = jnp.sum(piece.astype(F32), axis=0, keepdims=True)
    if hand_on is not None:
        copy.wait()


def products_of(weight, pieces, after, hand_on=None):
    vmem, anywhere = pl.BlockSpec(memory_space=pltpu.VMEM), pl.BlockSpec(memory_space=pl.ANY)
    half = jax.ShapeDtypeStruct((2 * GROUP_ROWS, LANES), F32)
    out = [pltpu.VMEM(half.shape, F32), half, jax.ShapeDtypeStruct((4, WIDTH), F32)]
    return pl.pallas_call(
        functools.partial(product_kernel, hand_on),
        out_shape=out + [jax.ShapeDtypeStruct((ROWS, WIDTH), BF16)] * (hand_on is not None),
        in_specs=[vmem] * 5 + [anywhere] * len(after),
        out_specs=[vmem] * 3 + [anywhere] * (hand_on is not None),
        scratch_shapes=[pltpu.SemaphoreType.DMA(())] * (hand_on is not None),
        compiler_params=pltpu.CompilerParams(vmem_limit_bytes=6 * 2**20),
        cost_estimate=pl.CostEstimate(flops=1_300_000_000, bytes_accessed=8_000_000, transcendentals=0),
        name="products",
    )(weight, *pieces, *after)


def slot_kernel(count, gather_rows, keep, place_ref, blocks_ref, *refs):
    if gather_rows:
        rows_ref, out_ref, picked, sems = refs[-4:] if keep else (refs[-1], *refs[-4:-1])
        copies = [
            pltpu.make_async_copy(refs[k], rows_ref.at[pl.ds(k * 2 * GROUP_ROWS, 2 * GROUP_ROWS), :], sems.at[k])
            for k in range(8)
        ]
        for copy in copies:
            copy.start()
        for copy in copies:
            copy.wait()
    else:
        rows_ref, (out_ref, picked) = refs[0], refs[-2:]

    @pl.loop(0, count)
    def _(b):
        base = blocks_ref[b] * BLOCK

        @pl.loop(0, BLOCK, step=UNROLL)
        def _(start):
            held = []
            for i in range(UNROLL):
                where = pl.multiple_of(place_ref[base + start + i], 2)
                held.append(rows_ref[pl.ds(where, 2), :])
            for i in range(UNROLL):
                picked[pl.ds(pl.multiple_of(2 * start, 2) + 2 * i, 2), :] = held[i]

        left, right = load_turned(picked, 0, BLOCK)
        out_ref[b, 0:LANES, :] = left
        out_ref[b, LANES:HID, :] = right


def to_slot_order(place, blocks, rows, after, keep=False):
    count = blocks.shape[0]
    vmem, anywhere = pl.BlockSpec(memory_space=pltpu.VMEM), pl.BlockSpec(memory_space=pl.ANY)
    out = [pltpu.VMEM((count, HID, BLOCK), F32)]
    whole = len(rows) == 1
    scratch = [pltpu.VMEM((2 * BLOCK, LANES), F32)] + [pltpu.SemaphoreType.DMA((8,))] * (not whole)
    if keep:
        out.insert(0, pltpu.VMEM((2 * SLOTS, LANES), F32))
    elif not whole:
        scratch.append(pltpu.VMEM((2 * SLOTS, LANES), F32))
    return pl.pallas_call(
        functools.partial(slot_kernel, count, not whole, keep),
        out_shape=out,
        in_specs=[pl.BlockSpec(memory_space=pltpu.SMEM)] * 2
        + [vmem if whole else anywhere] * len(rows)
        + [anywhere] * len(after),
        out_specs=[vmem] * len(out),
        scratch_shapes=scratch,
        compiler_params=pltpu.CompilerParams(vmem_limit_bytes=(5 if whole else 50) * 2**20),
        cost_estimate=pl.CostEstimate(flops=0, bytes_accessed=8_000_000 * count, transcendentals=0),
        name="slot_rows",
    )(place, blocks, *rows, *after)


def weight_kernel(first, mine_ref, theirs_ref, *refs):
    pieces = refs[:4]
    out_mine, out_theirs, held, sems = refs[-4:]
    copies = [
        pltpu.make_async_copy(piece, held.at[pl.ds(k * ROWS, ROWS), :], sems.at[k]) for k, piece in enumerate(pieces)
    ]
    for copy in copies:
        copy.start()
    for copy in copies:
        copy.wait()
    act = jnp.concatenate([mine_ref[...], theirs_ref[...]], axis=0)
    for n in range(0, WIDTH, 256):
        columns = slice(n, n + 256)
        term = jnp.dot(act, held[:, columns], preferred_element_type=F32)
        out_mine[:, columns] = term[:HID] if first else refs[4][:, columns] + term[:HID]
        out_theirs[:, columns] = term[HID:] if first else refs[5][:, columns] + term[HID:]


def weight_term(mine, theirs, pieces, totals, after):
    vmem = pl.BlockSpec(memory_space=pltpu.VMEM)
    return pl.pallas_call(
        functools.partial(weight_kernel, not totals),
        out_shape=[jax.ShapeDtypeStruct((HID, WIDTH), F32)] * 2,
        in_specs=[vmem] * 2 + [pl.BlockSpec(memory_space=pl.ANY)] * 4 + [vmem] * len(totals)
        + [pl.BlockSpec(memory_space=pl.ANY)] * len(after),
        out_specs=[vmem] * 2,
        scratch_shapes=[pltpu.VMEM((GROUP_ROWS, WIDTH), BF16), pltpu.SemaphoreType.DMA((4,))],
        compiler_params=pltpu.CompilerParams(vmem_limit_bytes=6 * 2**20),
        cost_estimate=pl.CostEstimate(flops=1_300_000_000, bytes_accessed=8_000_000, transcendentals=0),
        name="weight_term",
    )(mine, theirs, *pieces, *totals, *after)


def gelu_parts(pre):
    value = pre.astype(F32)
    cdf = 0.5 * (1.0 + jax.scipy.special.erf(value * 0.7071067811865476))
    activated = value * cdf
    slope = cdf + value * jnp.exp(-0.5 * value * value) * 0.3989422804014327
    return activated, slope


def body(grad_seq, positions, pre_act, w_out):
    me = lax.axis_index("text")
    place = 2 * (arrival_place(positions // ROWS, me) * ROWS + positions % ROWS)
    piece_of = arrival_place(jnp.arange(N_TEXT, dtype=jnp.int32), me)

    activated, slope = gelu_parts(pre_act.T)
    act_all = lax.all_gather(activated.astype(BF16), "tile", axis=0)
    swap = lambda value: lax.ppermute(value, "text", SWAP)
    send = lambda value, perm: lax.ppermute(value, "text", perm)
    weight = jnp.concatenate([w_out, swap(w_out)], axis=0)

    got = {(0, 0): grad_seq, (1, 0): send(grad_seq, FIRST_UP), (3, 0): send(grad_seq, FIRST_DOWN)}
    got[0, 1], got[0, 3] = send(grad_seq, SECOND_UP), send(grad_seq, SECOND_DOWN)
    got[2, 0] = send(got[1, 0], FIRST_UP)
    for first in (1, 3, 2):
        got[first, 1], got[first, 3] = send(got[first, 0], SECOND_UP), send(got[first, 0], SECOND_DOWN)
    act_mine, act_theirs, late_piece = act_in_arrival_order(place, act_all, got[3, 3])
    act_theirs = swap(act_theirs)
    mine, theirs, sums = [], [], []
    for g in range(GROUPS):
        pieces = [got[key] for key in ARRIVAL[4 * g:4 * g + 4]]
        kept, sent, part, *handed = products_of(weight, pieces, [], {0: 3, 1: 1}.get(g))
        if g == 0:
            got[0, 2] = send(handed[0], SECOND_UP)
        if g == 1:
            got[1, 2] = send(handed[0], SECOND_UP)
            got[3, 2], got[2, 2] = send(late_piece, SECOND_DOWN), send(got[2, 3], SECOND_DOWN)
        mine.append(kept)
        theirs.append(swap(sent))
        sums.append(part)
    groups = [[got[key] for key in ARRIVAL[4 * g:4 * g + 4]] for g in range(GROUPS)]
    tile = lax.axis_index("tile")
    parts = mine + theirs

    def slots(steps, rows, after, keep=False):
        return to_slot_order(place, (tile + jnp.array(steps, jnp.int32)) % N_TILE, rows, after, keep)

    rows, across = slots([4], parts, [], keep=True)
    (third,) = slots([3, 5], [rows], [across])
    up = lambda value: lax.ppermute(value.astype(BF16), "tile", TILE_UP)
    down = lambda value: lax.ppermute(value.astype(BF16), "tile", TILE_DOWN)
    rise, fall = up(across[0, :HALF]), down(across[0, HALF:])
    (second,) = slots([2, 6], parts, [rise])
    up3 = jnp.concatenate([rise.astype(F32) + third[0, :HALF], third[0, HALF:]], axis=0)
    down3 = jnp.concatenate([third[1, :HALF], fall.astype(F32) + third[1, HALF:]], axis=0)
    rise, fall = up(up3), down(down3)
    (nearest,) = slots([1, 7, 0], parts, [rise])
    rise, fall = up(rise.astype(F32) + second[0]), down(fall.astype(F32) + second[1])
    hop = rise
    rise, fall = up(rise.astype(F32) + nearest[0]), down(fall.astype(F32) + nearest[1])
    grad_pre = (nearest[2] + rise.astype(F32) + fall.astype(F32)) * lax.optimization_barrier(slope)
    totals = []
    for g in range(GROUPS):
        totals = weight_term(act_mine[g], act_theirs[g], groups[g], totals, [hop] if g == 1 else [])
    grad_w = totals[0] + swap(totals[1])
    sums = jnp.concatenate(sums, axis=0)
    sums = jnp.concatenate([sums, swap(sums)], axis=0)
    grad_bias = jnp.sum(sums[piece_of], axis=0)
    return grad_pre.T, grad_w, grad_bias


def solution(mesh):
    in_specs = (P("text", "tile"), P(), P("tile", "text"), P("text", "tile"))
    out_specs = (P("tile", "text"), P("text", "tile"), P("tile"))
    return jax.shard_map(body, mesh=mesh, in_specs=in_specs, out_specs=out_specs, check_vma=False)
```

```python
import functools

import jax
import jax.numpy as jnp
from jax import lax
from jax.experimental import pallas as pl
from jax.experimental.pallas import tpu as pltpu
from jax.sharding import PartitionSpec as P

SIDE = 4
N_TEXT = 2 * SIDE * SIDE
N_TILE = 8
ROWS = 320
HID = 160
BLOCK = 1280
SLOTS = 10240
WIDTH = 1024
HALF = HID // 2
LANES = 128
GROUPS = 4
GROUP_ROWS = 4 * ROWS
UNROLL = 32
F32 = jnp.float32
BF16 = jnp.bfloat16


def plane_perm(step0, step1):
    pairs = []
    for y in range(SIDE):
        for x in range(SIDE):
            for core, (dy, dx) in ((0, step0), (1, step1)):
                target = (((y + dy) % SIDE) * SIDE + (x + dx) % SIDE) * 2 + core
                pairs.append(((y * SIDE + x) * 2 + core, target))
    return pairs


FIRST_UP = plane_perm((0, 1), (1, 0))
FIRST_DOWN = plane_perm((0, -1), (-1, 0))
SECOND_UP = plane_perm((1, 0), (0, 1))
SECOND_DOWN = plane_perm((-1, 0), (0, -1))
ARRIVAL = [(0, 0), (1, 0), (3, 0), (0, 1), (0, 3), (1, 1), (2, 0), (3, 1), (1, 3), (3, 3), (0, 2), (2, 1), (2, 3), (1, 2), (3, 2), (2, 2)]
SWAP = [(i, i ^ 1) for i in range(N_TEXT)]
TILE_UP = [(i, (i + 1) % N_TILE) for i in range(N_TILE)]
TILE_DOWN = [(i, (i - 1) % N_TILE) for i in range(N_TILE)]


def arrival_place(device, me):
    core, x, y = device & 1, (device >> 1) & 3, device >> 3
    my_core, my_x, my_y = me & 1, (me >> 1) & 3, me >> 3
    dx, dy = (my_x - x) & 3, (my_y - y) & 3
    first = jnp.where(core == 0, dx, dy)
    second = jnp.where(core == 0, dy, dx)
    codes = [sum(ARRIVAL.index((i, j)) << (4 * i) for i in range(SIDE)) for j in range(SIDE)]
    code = jnp.where(second == 0, codes[0], jnp.where(second == 1, codes[1], jnp.where(second == 2, codes[2], codes[3])))
    return (core ^ my_core) * 16 + ((code >> (4 * first)) & 15)


def store_rows(ref, start, value):
    count = value.shape[0]
    ref[pl.ds(start, count, stride=2), :] = value[:, :LANES]
    ref[pl.ds(start + 1, count, stride=2), 0:HID - LANES] = value[:, LANES:]


def load_turned(ref, start, count):
    left = ref[pl.ds(start, count, stride=2), :].T
    right = ref[pl.ds(start + 1, count, stride=2), :].T
    return left, right[0:HID - LANES]


def act_kernel(place_ref, act_ref, piece_ref, mine_ref, theirs_ref, next_ref, rows, turned, sem):
    block = pl.program_id(0)
    copy = pltpu.make_async_copy(piece_ref, next_ref, sem)

    @pl.when(block == 0)
    def _():
        copy.start()

    store_rows(turned, 0, act_ref[0].astype(F32).T)

    @pl.loop(0, BLOCK, step=UNROLL)
    def _(start):
        held = [turned[pl.ds(pl.multiple_of(2 * start, 2) + 2 * i, 2), :] for i in range(UNROLL)]
        for i in range(UNROLL):
            where = pl.multiple_of(place_ref[block * BLOCK + start + i], 2)
            rows[pl.ds(where, 2), :] = held[i]

    @pl.when(block == N_TILE - 1)
    def _():
        for group in range(2 * GROUPS):
            left, right = load_turned(rows, group * 2 * GROUP_ROWS, GROUP_ROWS)
            out_ref = (mine_ref, theirs_ref)[group // GROUPS]
            out_ref[group % GROUPS, 0:LANES, :] = left.astype(BF16)
            out_ref[group % GROUPS, LANES:HID, :] = right.astype(BF16)
        copy.wait()


def act_in_arrival_order(place, act, piece):
    return pl.pallas_call(
        act_kernel,
        out_shape=[jax.ShapeDtypeStruct((GROUPS, HID, GROUP_ROWS), BF16)] * 2
        + [jax.ShapeDtypeStruct(piece.shape, piece.dtype)],
        grid_spec=pltpu.PrefetchScalarGridSpec(
            num_scalar_prefetch=1,
            grid=(N_TILE,),
            in_specs=[
                pl.BlockSpec((1, HID, BLOCK), lambda i, place: (i, 0, 0)),
                pl.BlockSpec(memory_space=pl.ANY),
            ],
            out_specs=[pl.BlockSpec((GROUPS, HID, GROUP_ROWS), lambda i, place: (0, 0, 0), pipeline_mode=pl.Buffered(1))] * 2
            + [pl.BlockSpec(memory_space=pl.ANY)],
            scratch_shapes=[
                pltpu.VMEM((2 * SLOTS, LANES), F32),
                pltpu.VMEM((2 * BLOCK, LANES), F32),
                pltpu.SemaphoreType.DMA(()),
            ],
        ),
        compiler_params=pltpu.CompilerParams(vmem_limit_bytes=17 * 2**20),
        cost_estimate=pl.CostEstimate(flops=0, bytes_accessed=70_000_000, transcendentals=0),
        name="act_rows",
    )(place, act, piece)


def product_kernel(hand_on, weight_ref, *refs):
    pieces = refs[:4]
    if hand_on is None:
        mine_ref, theirs_ref, sums_ref = refs[-3:]
    else:
        mine_ref, theirs_ref, sums_ref, next_ref, sem = refs[-5:]
        copy = pltpu.make_async_copy(pieces[hand_on], next_ref, sem)
        copy.start()
    for k in range(4):
        piece = pieces[k][...]
        term = lax.dot_general(piece, weight_ref[...], (((1,), (1,)), ((), ())), preferred_element_type=F32)
        store_rows(mine_ref, 2 * k * ROWS, term[:, :HID])
        store_rows(theirs_ref, 2 * k * ROWS, term[:, HID:])
        sums_ref[k:k + 1, :] = jnp.sum(piece.astype(F32), axis=0, keepdims=True)
    if hand_on is not None:
        copy.wait()


def products_of(weight, pieces, after, hand_on=None):
    vmem, anywhere = pl.BlockSpec(memory_space=pltpu.VMEM), pl.BlockSpec(memory_space=pl.ANY)
    half = jax.ShapeDtypeStruct((2 * GROUP_ROWS, LANES), F32)
    out = [pltpu.VMEM(half.shape, F32), half, jax.ShapeDtypeStruct((4, WIDTH), F32)]
    return pl.pallas_call(
        functools.partial(product_kernel, hand_on),
        out_shape=out + [jax.ShapeDtypeStruct((ROWS, WIDTH), BF16)] * (hand_on is not None),
        in_specs=[vmem] * 5 + [anywhere] * len(after),
        out_specs=[vmem] * 3 + [anywhere] * (hand_on is not None),
        scratch_shapes=[pltpu.SemaphoreType.DMA(())] * (hand_on is not None),
        compiler_params=pltpu.CompilerParams(vmem_limit_bytes=6 * 2**20),
        cost_estimate=pl.CostEstimate(flops=1_300_000_000, bytes_accessed=8_000_000, transcendentals=0),
        name="products",
    )(weight, *pieces, *after)


def slot_kernel(count, gather_rows, keep, place_ref, blocks_ref, *refs):
    if gather_rows:
        rows_ref, out_ref, picked, sems = refs[-4:] if keep else (refs[-1], *refs[-4:-1])
        copies = [
            pltpu.make_async_copy(refs[k], rows_ref.at[pl.ds(k * 2 * GROUP_ROWS, 2 * GROUP_ROWS), :], sems.at[k])
            for k in range(8)
        ]
        for copy in copies:
            copy.start()
        for copy in copies:
            copy.wait()
    else:
        rows_ref, (out_ref, picked) = refs[0], refs[-2:]

    @pl.loop(0, count)
    def _(b):
        base = blocks_ref[b] * BLOCK

        @pl.loop(0, BLOCK, step=UNROLL)
        def _(start):
            held = []
            for i in range(UNROLL):
                where = pl.multiple_of(place_ref[base + start + i], 2)
                held.append(rows_ref[pl.ds(where, 2), :])
            for i in range(UNROLL):
                picked[pl.ds(pl.multiple_of(2 * start, 2) + 2 * i, 2), :] = held[i]

        left, right = load_turned(picked, 0, BLOCK)
        out_ref[b, 0:LANES, :] = left
        out_ref[b, LANES:HID, :] = right


def to_slot_order(place, blocks, rows, after, keep=False):
    count = blocks.shape[0]
    vmem, anywhere = pl.BlockSpec(memory_space=pltpu.VMEM), pl.BlockSpec(memory_space=pl.ANY)
    out = [pltpu.VMEM((count, HID, BLOCK), F32)]
    whole = len(rows) == 1
    scratch = [pltpu.VMEM((2 * BLOCK, LANES), F32)] + [pltpu.SemaphoreType.DMA((8,))] * (not whole)
    if keep:
        out.insert(0, pltpu.VMEM((2 * SLOTS, LANES), F32))
    elif not whole:
        scratch.append(pltpu.VMEM((2 * SLOTS, LANES), F32))
    return pl.pallas_call(
        functools.partial(slot_kernel, count, not whole, keep),
        out_shape=out,
        in_specs=[pl.BlockSpec(memory_space=pltpu.SMEM)] * 2
        + [vmem if whole else anywhere] * len(rows)
        + [anywhere] * len(after),
        out_specs=[vmem] * len(out),
        scratch_shapes=scratch,
        compiler_params=pltpu.CompilerParams(vmem_limit_bytes=(5 if whole else 50) * 2**20),
        cost_estimate=pl.CostEstimate(flops=0, bytes_accessed=8_000_000 * count, transcendentals=0),
        name="slot_rows",
    )(place, blocks, *rows, *after)


def hop_kernel(which, fresh, terms_ref, come_ref, out_ref):
    term, come = terms_ref[which], come_ref[...].astype(F32)
    if fresh is None:
        out_ref[...] = (term + come).astype(BF16)
        return
    added = slice(HALF, HID) if fresh == 0 else slice(0, HALF)
    out_ref[added, :] = (term[added] + come).astype(BF16)
    out_ref[fresh:fresh + HALF, :] = term[fresh:fresh + HALF].astype(BF16)


def hop(which, fresh, terms, come):
    vmem = pl.BlockSpec(memory_space=pltpu.VMEM)
    return pl.pallas_call(
        functools.partial(hop_kernel, which, fresh),
        out_shape=jax.ShapeDtypeStruct((HID, BLOCK), BF16),
        in_specs=[vmem] * 2,
        out_specs=vmem,
        compiler_params=pltpu.CompilerParams(vmem_limit_bytes=4 * 2**20),
        cost_estimate=pl.CostEstimate(flops=0, bytes_accessed=1_500_000, transcendentals=0),
        name="hop_sum",
    )(terms, come)


def weight_kernel(first, mine_ref, theirs_ref, *refs):
    pieces = refs[:4]
    out_mine, out_theirs, held, sems = refs[-4:]
    copies = [
        pltpu.make_async_copy(piece, held.at[pl.ds(k * ROWS, ROWS), :], sems.at[k]) for k, piece in enumerate(pieces)
    ]
    for copy in copies:
        copy.start()
    for copy in copies:
        copy.wait()
    act = jnp.concatenate([mine_ref[...], theirs_ref[...]], axis=0)
    for n in range(0, WIDTH, 256):
        columns = slice(n, n + 256)
        term = jnp.dot(act, held[:, columns], preferred_element_type=F32)
        out_mine[:, columns] = term[:HID] if first else refs[4][:, columns] + term[:HID]
        out_theirs[:, columns] = term[HID:] if first else refs[5][:, columns] + term[HID:]


def weight_term(mine, theirs, pieces, totals, after):
    vmem = pl.BlockSpec(memory_space=pltpu.VMEM)
    return pl.pallas_call(
        functools.partial(weight_kernel, not totals),
        out_shape=[jax.ShapeDtypeStruct((HID, WIDTH), F32)] * 2,
        in_specs=[vmem] * 2 + [pl.BlockSpec(memory_space=pl.ANY)] * 4 + [vmem] * len(totals)
        + [pl.BlockSpec(memory_space=pl.ANY)] * len(after),
        out_specs=[vmem] * 2,
        scratch_shapes=[pltpu.VMEM((GROUP_ROWS, WIDTH), BF16), pltpu.SemaphoreType.DMA((4,))],
        compiler_params=pltpu.CompilerParams(vmem_limit_bytes=6 * 2**20),
        cost_estimate=pl.CostEstimate(flops=1_300_000_000, bytes_accessed=8_000_000, transcendentals=0),
        name="weight_term",
    )(mine, theirs, *pieces, *totals, *after)


def gelu_parts(pre):
    value = pre.astype(F32)
    cdf = 0.5 * (1.0 + jax.scipy.special.erf(value * 0.7071067811865476))
    activated = value * cdf
    slope = cdf + value * jnp.exp(-0.5 * value * value) * 0.3989422804014327
    return activated, slope


def body(grad_seq, positions, pre_act, w_out):
    me = lax.axis_index("text")
    place = 2 * (arrival_place(positions // ROWS, me) * ROWS + positions % ROWS)
    piece_of = arrival_place(jnp.arange(N_TEXT, dtype=jnp.int32), me)

    activated, slope = gelu_parts(pre_act.T)
    act_all = lax.all_gather(activated.astype(BF16), "tile", axis=0)
    swap = lambda value: lax.ppermute(value, "text", SWAP)
    send = lambda value, perm: lax.ppermute(value, "text", perm)
    weight = jnp.concatenate([w_out, swap(w_out)], axis=0)

    got = {(0, 0): grad_seq, (1, 0): send(grad_seq, FIRST_UP), (3, 0): send(grad_seq, FIRST_DOWN)}
    got[0, 1], got[0, 3] = send(grad_seq, SECOND_UP), send(grad_seq, SECOND_DOWN)
    got[2, 0] = send(got[1, 0], FIRST_UP)
    for first in (1, 2):
        got[first, 1], got[first, 3] = send(got[first, 0], SECOND_UP), send(got[first, 0], SECOND_DOWN)
    got[0, 2] = send(got[0, 1], SECOND_UP)
    first_products = products_of(weight, [got[key] for key in ARRIVAL[:4]], [], 2)
    got[3, 1], got[3, 3] = send(first_products[3], SECOND_UP), send(got[3, 0], SECOND_DOWN)
    act_mine, act_theirs, late_piece = act_in_arrival_order(place, act_all, got[3, 3])
    act_theirs = swap(act_theirs)
    mine, theirs, sums = [], [], []
    for g in range(GROUPS):
        pieces = [got[key] for key in ARRIVAL[4 * g:4 * g + 4]]
        kept, sent, part, *handed = first_products if g == 0 else products_of(weight, pieces, [], 1 if g == 1 else None)
        if g == 1:
            got[1, 2] = send(handed[0], SECOND_UP)
            got[3, 2], got[2, 2] = send(late_piece, SECOND_DOWN), send(got[2, 3], SECOND_DOWN)
        mine.append(kept)
        theirs.append(swap(sent))
        sums.append(part)
    groups = [[got[key] for key in ARRIVAL[4 * g:4 * g + 4]] for g in range(GROUPS)]
    tile = lax.axis_index("tile")
    parts = mine + theirs

    def slots(steps, rows, after, keep=False):
        return to_slot_order(place, (tile + jnp.array(steps, jnp.int32)) % N_TILE, rows, after, keep)

    rows, across = slots([4], parts, [], keep=True)
    (third,) = slots([3, 5], [rows], [across])
    up = lambda value: lax.ppermute(value.astype(BF16), "tile", TILE_UP)
    down = lambda value: lax.ppermute(value.astype(BF16), "tile", TILE_DOWN)
    rise, fall = up(across[0, :HALF]), down(across[0, HALF:])
    (second,) = slots([2, 6], parts, [rise])
    rise, fall = up(hop(0, HALF, third, rise)), down(hop(1, 0, third, fall))
    (nearest,) = slots([1, 7, 0], parts, [rise])
    rise, fall = up(hop(0, None, second, rise)), down(hop(1, None, second, fall))
    arrived = rise
    rise, fall = up(hop(0, None, nearest, rise)), down(hop(1, None, nearest, fall))
    grad_pre = (nearest[2] + rise.astype(F32) + fall.astype(F32)) * lax.optimization_barrier(slope)
    totals = []
    for g in range(GROUPS):
        totals = weight_term(act_mine[g], act_theirs[g], groups[g], totals, [arrived] if g == 1 else [])
    grad_w = totals[0] + swap(totals[1])
    sums = jnp.concatenate(sums, axis=0)
    sums = jnp.concatenate([sums, swap(sums)], axis=0)
    grad_bias = jnp.sum(sums[piece_of], axis=0)
    return grad_pre.T, grad_w, grad_bias


def solution(mesh):
    in_specs = (P("text", "tile"), P(), P("tile", "text"), P("text", "tile"))
    out_specs = (P("tile", "text"), P("text", "tile"), P("tile"))
    return jax.shard_map(body, mesh=mesh, in_specs=in_specs, out_specs=out_specs, check_vma=False)
```

```python
import functools

import jax
import jax.numpy as jnp
from jax import lax
from jax.experimental import pallas as pl
from jax.experimental.pallas import tpu as pltpu
from jax.sharding import PartitionSpec as P

SIDE = 4
N_TEXT = 2 * SIDE * SIDE
N_TILE = 8
ROWS = 320
HID = 160
BLOCK = 1280
SLOTS = 10240
WIDTH = 1024
HALF = HID // 2
LANES = 128
GROUPS = 4
GROUP_ROWS = 4 * ROWS
UNROLL = 32
F32 = jnp.float32
BF16 = jnp.bfloat16


def plane_perm(step0, step1):
    pairs = []
    for y in range(SIDE):
        for x in range(SIDE):
            for core, (dy, dx) in ((0, step0), (1, step1)):
                target = (((y + dy) % SIDE) * SIDE + (x + dx) % SIDE) * 2 + core
                pairs.append(((y * SIDE + x) * 2 + core, target))
    return pairs


FIRST_UP = plane_perm((0, 1), (1, 0))
FIRST_DOWN = plane_perm((0, -1), (-1, 0))
SECOND_UP = plane_perm((1, 0), (0, 1))
SECOND_DOWN = plane_perm((-1, 0), (0, -1))
ARRIVAL = [(0, 0), (1, 0), (3, 0), (0, 1), (0, 3), (1, 1), (2, 0), (3, 1), (1, 3), (3, 3), (0, 2), (2, 1), (2, 3), (1, 2), (3, 2), (2, 2)]
SWAP = [(i, i ^ 1) for i in range(N_TEXT)]
TILE_UP = [(i, (i + 1) % N_TILE) for i in range(N_TILE)]
TILE_DOWN = [(i, (i - 1) % N_TILE) for i in range(N_TILE)]


def arrival_place(device, me):
    core, x, y = device & 1, (device >> 1) & 3, device >> 3
    my_core, my_x, my_y = me & 1, (me >> 1) & 3, me >> 3
    dx, dy = (my_x - x) & 3, (my_y - y) & 3
    first = jnp.where(core == 0, dx, dy)
    second = jnp.where(core == 0, dy, dx)
    codes = [sum(ARRIVAL.index((i, j)) << (4 * i) for i in range(SIDE)) for j in range(SIDE)]
    code = jnp.where(second == 0, codes[0], jnp.where(second == 1, codes[1], jnp.where(second == 2, codes[2], codes[3])))
    return (core ^ my_core) * 16 + ((code >> (4 * first)) & 15)


def store_rows(ref, start, value):
    count = value.shape[0]
    ref[pl.ds(start, count, stride=2), :] = value[:, :LANES]
    ref[pl.ds(start + 1, count, stride=2), 0:HID - LANES] = value[:, LANES:]


def load_turned(ref, start, count):
    left = ref[pl.ds(start, count, stride=2), :].T
    right = ref[pl.ds(start + 1, count, stride=2), :].T
    return left, right[0:HID - LANES]


def act_kernel(place_ref, act_ref, piece_ref, mine_ref, theirs_ref, next_ref, rows, turned, sem):
    block = pl.program_id(0)
    copy = pltpu.make_async_copy(piece_ref, next_ref, sem)

    @pl.when(block == 0)
    def _():
        copy.start()

    store_rows(turned, 0, act_ref[0].astype(F32).T)

    @pl.loop(0, BLOCK, step=UNROLL)
    def _(start):
        held = [turned[pl.ds(pl.multiple_of(2 * start, 2) + 2 * i, 2), :] for i in range(UNROLL)]
        for i in range(UNROLL):
            where = pl.multiple_of(place_ref[block * BLOCK + start + i], 2)
            rows[pl.ds(where, 2), :] = held[i]

    @pl.when(block == N_TILE - 1)
    def _():
        for group in range(2 * GROUPS):
            left, right = load_turned(rows, group * 2 * GROUP_ROWS, GROUP_ROWS)
            out_ref = (mine_ref, theirs_ref)[group // GROUPS]
            out_ref[group % GROUPS, 0:LANES, :] = left.astype(BF16)
            out_ref[group % GROUPS, LANES:HID, :] = right.astype(BF16)
        copy.wait()


def act_in_arrival_order(place, act, piece):
    return pl.pallas_call(
        act_kernel,
        out_shape=[jax.ShapeDtypeStruct((GROUPS, HID, GROUP_ROWS), BF16)] * 2
        + [jax.ShapeDtypeStruct(piece.shape, piece.dtype)],
        grid_spec=pltpu.PrefetchScalarGridSpec(
            num_scalar_prefetch=1,
            grid=(N_TILE,),
            in_specs=[
                pl.BlockSpec((1, HID, BLOCK), lambda i, place: (i, 0, 0)),
                pl.BlockSpec(memory_space=pl.ANY),
            ],
            out_specs=[pl.BlockSpec((GROUPS, HID, GROUP_ROWS), lambda i, place: (0, 0, 0), pipeline_mode=pl.Buffered(1))] * 2
            + [pl.BlockSpec(memory_space=pl.ANY)],
            scratch_shapes=[
                pltpu.VMEM((2 * SLOTS, LANES), F32),
                pltpu.VMEM((2 * BLOCK, LANES), F32),
                pltpu.SemaphoreType.DMA(()),
            ],
        ),
        compiler_params=pltpu.CompilerParams(vmem_limit_bytes=17 * 2**20),
        cost_estimate=pl.CostEstimate(flops=0, bytes_accessed=70_000_000, transcendentals=0),
        name="act_rows",
    )(place, act, piece)


def product_kernel(hand_on, weight_ref, *refs):
    pieces = refs[:4]
    if hand_on is None:
        mine_ref, theirs_ref, sums_ref = refs[-3:]
    else:
        mine_ref, theirs_ref, sums_ref, next_ref, sem = refs[-5:]
        copy = pltpu.make_async_copy(pieces[hand_on], next_ref, sem)
        copy.start()
    for k in range(4):
        piece = pieces[k][...]
        term = lax.dot_general(piece, weight_ref[...], (((1,), (1,)), ((), ())), preferred_element_type=F32)
        store_rows(mine_ref, 2 * k * ROWS, term[:, :HID])
        store_rows(theirs_ref, 2 * k * ROWS, term[:, HID:])
        sums_ref[k:k + 1, :] = jnp.sum(piece.astype(F32), axis=0, keepdims=True)
    if hand_on is not None:
        copy.wait()


def products_of(weight, pieces, after, hand_on=None):
    vmem, anywhere = pl.BlockSpec(memory_space=pltpu.VMEM), pl.BlockSpec(memory_space=pl.ANY)
    half = jax.ShapeDtypeStruct((2 * GROUP_ROWS, LANES), F32)
    out = [pltpu.VMEM(half.shape, F32), half, jax.ShapeDtypeStruct((4, WIDTH), F32)]
    return pl.pallas_call(
        functools.partial(product_kernel, hand_on),
        out_shape=out + [jax.ShapeDtypeStruct((ROWS, WIDTH), BF16)] * (hand_on is not None),
        in_specs=[vmem] * 5 + [anywhere] * len(after),
        out_specs=[vmem] * 3 + [anywhere] * (hand_on is not None),
        scratch_shapes=[pltpu.SemaphoreType.DMA(())] * (hand_on is not None),
        compiler_params=pltpu.CompilerParams(vmem_limit_bytes=6 * 2**20),
        cost_estimate=pl.CostEstimate(flops=1_300_000_000, bytes_accessed=8_000_000, transcendentals=0),
        name="products",
    )(weight, *pieces, *after)


def slot_kernel(count, gather_rows, keep, place_ref, blocks_ref, *refs):
    if gather_rows:
        rows_ref, out_ref, picked, sems = refs[-4:] if keep else (refs[-1], *refs[-4:-1])
        copies = [
            pltpu.make_async_copy(refs[k], rows_ref.at[pl.ds(k * 2 * GROUP_ROWS, 2 * GROUP_ROWS), :], sems.at[k])
            for k in range(8)
        ]
        for copy in copies:
            copy.start()
        for copy in copies:
            copy.wait()
    else:
        rows_ref, (out_ref, picked) = refs[0], refs[-2:]

    @pl.loop(0, count)
    def _(b):
        base = blocks_ref[b] * BLOCK

        @pl.loop(0, BLOCK, step=UNROLL)
        def _(start):
            held = []
            for i in range(UNROLL):
                where = pl.multiple_of(place_ref[base + start + i], 2)
                held.append(rows_ref[pl.ds(where, 2), :])
            for i in range(UNROLL):
                picked[pl.ds(pl.multiple_of(2 * start, 2) + 2 * i, 2), :] = held[i]

        left, right = load_turned(picked, 0, BLOCK)
        out_ref[b, 0:LANES, :] = left
        out_ref[b, LANES:HID, :] = right


def to_slot_order(place, blocks, rows, after, keep=False):
    count = blocks.shape[0]
    vmem, anywhere = pl.BlockSpec(memory_space=pltpu.VMEM), pl.BlockSpec(memory_space=pl.ANY)
    out = [pltpu.VMEM((count, HID, BLOCK), F32)]
    whole = len(rows) == 1
    scratch = [pltpu.VMEM((2 * BLOCK, LANES), F32)] + [pltpu.SemaphoreType.DMA((8,))] * (not whole)
    if keep:
        out.insert(0, pltpu.VMEM((2 * SLOTS, LANES), F32))
    elif not whole:
        scratch.append(pltpu.VMEM((2 * SLOTS, LANES), F32))
    return pl.pallas_call(
        functools.partial(slot_kernel, count, not whole, keep),
        out_shape=out,
        in_specs=[pl.BlockSpec(memory_space=pltpu.SMEM)] * 2
        + [vmem if whole else anywhere] * len(rows)
        + [anywhere] * len(after),
        out_specs=[vmem] * len(out),
        scratch_shapes=scratch,
        compiler_params=pltpu.CompilerParams(vmem_limit_bytes=(5 if whole else 50) * 2**20),
        cost_estimate=pl.CostEstimate(flops=0, bytes_accessed=8_000_000 * count, transcendentals=0),
        name="slot_rows",
    )(place, blocks, *rows, *after)


def hop_kernel(which, fresh, terms_ref, come_ref, *refs):
    out_ref = refs[-1]
    term, come = terms_ref[which], come_ref[...].astype(F32)
    if fresh is None:
        out_ref[...] = (term + come).astype(BF16)
        return
    added = slice(HALF, HID) if fresh == 0 else slice(0, HALF)
    out_ref[added, :] = (term[added] + come).astype(BF16)
    out_ref[fresh:fresh + HALF, :] = term[fresh:fresh + HALF].astype(BF16)


def hop(which, fresh, terms, come, after=()):
    vmem = pl.BlockSpec(memory_space=pltpu.VMEM)
    return pl.pallas_call(
        functools.partial(hop_kernel, which, fresh),
        out_shape=jax.ShapeDtypeStruct((HID, BLOCK), BF16),
        in_specs=[vmem] * 2 + [pl.BlockSpec(memory_space=pl.ANY)] * len(after),
        out_specs=vmem,
        compiler_params=pltpu.CompilerParams(vmem_limit_bytes=4 * 2**20),
        cost_estimate=pl.CostEstimate(flops=0, bytes_accessed=1_500_000, transcendentals=0),
        name="hop_sum",
    )(terms, come, *after)


def weight_kernel(first, mine_ref, theirs_ref, *refs):
    pieces = refs[:4]
    out_mine, out_theirs, held, sems = refs[-4:]
    copies = [
        pltpu.make_async_copy(piece, held.at[pl.ds(k * ROWS, ROWS), :], sems.at[k]) for k, piece in enumerate(pieces)
    ]
    for copy in copies:
        copy.start()
    for copy in copies:
        copy.wait()
    act = jnp.concatenate([mine_ref[...], theirs_ref[...]], axis=0)
    for n in range(0, WIDTH, 256):
        columns = slice(n, n + 256)
        term = jnp.dot(act, held[:, columns], preferred_element_type=F32)
        out_mine[:, columns] = term[:HID] if first else refs[4][:, columns] + term[:HID]
        out_theirs[:, columns] = term[HID:] if first else refs[5][:, columns] + term[HID:]


def weight_term(mine, theirs, pieces, totals, after):
    vmem = pl.BlockSpec(memory_space=pltpu.VMEM)
    return pl.pallas_call(
        functools.partial(weight_kernel, not totals),
        out_shape=[jax.ShapeDtypeStruct((HID, WIDTH), F32)] * 2,
        in_specs=[vmem] * 2 + [pl.BlockSpec(memory_space=pl.ANY)] * 4 + [vmem] * len(totals)
        + [pl.BlockSpec(memory_space=pl.ANY)] * len(after),
        out_specs=[vmem] * 2,
        scratch_shapes=[pltpu.VMEM((GROUP_ROWS, WIDTH), BF16), pltpu.SemaphoreType.DMA((4,))],
        compiler_params=pltpu.CompilerParams(vmem_limit_bytes=6 * 2**20),
        cost_estimate=pl.CostEstimate(flops=1_300_000_000, bytes_accessed=8_000_000, transcendentals=0),
        name="weight_term",
    )(mine, theirs, *pieces, *totals, *after)


def gelu_parts(pre):
    value = pre.astype(F32)
    cdf = 0.5 * (1.0 + jax.scipy.special.erf(value * 0.7071067811865476))
    activated = value * cdf
    slope = cdf + value * jnp.exp(-0.5 * value * value) * 0.3989422804014327
    return activated, slope


def body(grad_seq, positions, pre_act, w_out):
    me = lax.axis_index("text")
    place = 2 * (arrival_place(positions // ROWS, me) * ROWS + positions % ROWS)
    piece_of = arrival_place(jnp.arange(N_TEXT, dtype=jnp.int32), me)

    activated, slope = gelu_parts(pre_act.T)
    act_all = lax.all_gather(activated.astype(BF16), "tile", axis=0)
    swap = lambda value: lax.ppermute(value, "text", SWAP)
    send = lambda value, perm: lax.ppermute(value, "text", perm)
    weight = jnp.concatenate([w_out, swap(w_out)], axis=0)

    got = {(0, 0): grad_seq, (1, 0): send(grad_seq, FIRST_UP), (3, 0): send(grad_seq, FIRST_DOWN)}
    got[0, 1], got[0, 3] = send(grad_seq, SECOND_UP), send(grad_seq, SECOND_DOWN)
    got[2, 0] = send(got[1, 0], FIRST_UP)
    for first in (1, 2):
        got[first, 1], got[first, 3] = send(got[first, 0], SECOND_UP), send(got[first, 0], SECOND_DOWN)
    got[0, 2] = send(got[0, 1], SECOND_UP)
    first_products = products_of(weight, [got[key] for key in ARRIVAL[:4]], [], 2)
    got[3, 1], got[3, 3] = send(first_products[3], SECOND_UP), send(got[3, 0], SECOND_DOWN)
    act_mine, act_theirs, late_piece = act_in_arrival_order(place, act_all, got[3, 3])
    act_theirs = swap(act_theirs)
    mine, theirs, sums = [], [], []
    for g in range(GROUPS):
        pieces = [got[key] for key in ARRIVAL[4 * g:4 * g + 4]]
        kept, sent, part, *handed = first_products if g == 0 else products_of(weight, pieces, [], 1 if g == 1 else None)
        if g == 1:
            got[1, 2] = send(handed[0], SECOND_UP)
            got[3, 2], got[2, 2] = send(late_piece, SECOND_DOWN), send(got[2, 3], SECOND_DOWN)
        mine.append(kept)
        theirs.append(swap(sent))
        sums.append(part)
    groups = [[got[key] for key in ARRIVAL[4 * g:4 * g + 4]] for g in range(GROUPS)]
    tile = lax.axis_index("tile")
    parts = mine + theirs

    def slots(steps, rows, after, keep=False):
        return to_slot_order(place, (tile + jnp.array(steps, jnp.int32)) % N_TILE, rows, after, keep)

    rows, across = slots([4], parts, [], keep=True)
    (middle,) = slots([3, 5, 2, 6], [rows], [across])
    up = lambda value: lax.ppermute(value.astype(BF16), "tile", TILE_UP)
    down = lambda value: lax.ppermute(value.astype(BF16), "tile", TILE_DOWN)
    rise, fall = up(across[0, :HALF]), down(across[0, HALF:])
    (nearest,) = slots([1, 7, 0], parts, [rise])
    rise, fall = up(hop(0, HALF, middle, rise)), down(hop(1, 0, middle, fall))
    arrived = [rise]
    totals = weight_term(act_mine[0], act_theirs[0], groups[0], [], [])
    rise, fall = up(hop(2, None, middle, rise, totals[:1])), down(hop(3, None, middle, fall))
    arrived.append(rise)
    rise, fall = up(hop(0, None, nearest, rise)), down(hop(1, None, nearest, fall))
    grad_pre = (nearest[2] + rise.astype(F32) + fall.astype(F32)) * lax.optimization_barrier(slope)
    for g in range(1, GROUPS):
        totals = weight_term(act_mine[g], act_theirs[g], groups[g], totals, arrived[1:] if g == 1 else [])
    grad_w = totals[0] + swap(totals[1])
    sums = jnp.concatenate(sums, axis=0)
    sums = jnp.concatenate([sums, swap(sums)], axis=0)
    grad_bias = jnp.sum(sums[piece_of], axis=0)
    return grad_pre.T, grad_w, grad_bias


def solution(mesh):
    in_specs = (P("text", "tile"), P(), P("tile", "text"), P("text", "tile"))
    out_specs = (P("tile", "text"), P("text", "tile"), P("tile"))
    return jax.shard_map(body, mesh=mesh, in_specs=in_specs, out_specs=out_specs, check_vma=False)
```

```python
import functools

import jax
import jax.numpy as jnp
from jax import lax
from jax.experimental import pallas as pl
from jax.experimental.pallas import tpu as pltpu
from jax.sharding import PartitionSpec as P

SIDE = 4
N_TEXT = 2 * SIDE * SIDE
N_TILE = 8
ROWS = 320
HID = 160
BLOCK = 1280
SLOTS = 10240
WIDTH = 1024
HALF = HID // 2
LANES = 128
GROUPS = 4
GROUP_ROWS = 4 * ROWS
UNROLL = 32
F32 = jnp.float32
BF16 = jnp.bfloat16


def plane_perm(step0, step1):
    pairs = []
    for y in range(SIDE):
        for x in range(SIDE):
            for core, (dy, dx) in ((0, step0), (1, step1)):
                target = (((y + dy) % SIDE) * SIDE + (x + dx) % SIDE) * 2 + core
                pairs.append(((y * SIDE + x) * 2 + core, target))
    return pairs


FIRST_UP = plane_perm((0, 1), (1, 0))
FIRST_DOWN = plane_perm((0, -1), (-1, 0))
SECOND_UP = plane_perm((1, 0), (0, 1))
SECOND_DOWN = plane_perm((-1, 0), (0, -1))
ARRIVAL = [(0, 0), (1, 0), (3, 0), (0, 1), (0, 3), (1, 1), (2, 0), (3, 1), (1, 3), (3, 3), (0, 2), (2, 1), (2, 3), (1, 2), (3, 2), (2, 2)]
SWAP = [(i, i ^ 1) for i in range(N_TEXT)]
TILE_UP = [(i, (i + 1) % N_TILE) for i in range(N_TILE)]
TILE_DOWN = [(i, (i - 1) % N_TILE) for i in range(N_TILE)]


def arrival_place(device, me):
    core, x, y = device & 1, (device >> 1) & 3, device >> 3
    my_core, my_x, my_y = me & 1, (me >> 1) & 3, me >> 3
    dx, dy = (my_x - x) & 3, (my_y - y) & 3
    first = jnp.where(core == 0, dx, dy)
    second = jnp.where(core == 0, dy, dx)
    codes = [sum(ARRIVAL.index((i, j)) << (4 * i) for i in range(SIDE)) for j in range(SIDE)]
    code = jnp.where(second == 0, codes[0], jnp.where(second == 1, codes[1], jnp.where(second == 2, codes[2], codes[3])))
    return (core ^ my_core) * 16 + ((code >> (4 * first)) & 15)


def store_rows(ref, start, value):
    count = value.shape[0]
    ref[pl.ds(start, count, stride=2), :] = value[:, :LANES]
    ref[pl.ds(start + 1, count, stride=2), 0:HID - LANES] = value[:, LANES:]


def load_turned(ref, start, count):
    left = ref[pl.ds(start, count, stride=2), :].T
    right = ref[pl.ds(start + 1, count, stride=2), :].T
    return left, right[0:HID - LANES]


def act_kernel(place_ref, act_ref, piece_ref, mine_ref, theirs_ref, next_ref, rows, turned, sem):
    block = pl.program_id(0)
    copy = pltpu.make_async_copy(piece_ref, next_ref, sem)

    @pl.when(block == 0)
    def _():
        copy.start()

    store_rows(turned, 0, act_ref[0].astype(F32).T)

    @pl.loop(0, BLOCK, step=UNROLL)
    def _(start):
        held = [turned[pl.ds(pl.multiple_of(2 * start, 2) + 2 * i, 2), :] for i in range(UNROLL)]
        for i in range(UNROLL):
            where = pl.multiple_of(place_ref[block * BLOCK + start + i], 2)
            rows[pl.ds(where, 2), :] = held[i]

    @pl.when(block == N_TILE - 1)
    def _():
        for group in range(2 * GROUPS):
            left, right = load_turned(rows, group * 2 * GROUP_ROWS, GROUP_ROWS)
            out_ref = (mine_ref, theirs_ref)[group // GROUPS]
            out_ref[group % GROUPS, 0:LANES, :] = left.astype(BF16)
            out_ref[group % GROUPS, LANES:HID, :] = right.astype(BF16)
        copy.wait()


def act_in_arrival_order(place, act, piece):
    return pl.pallas_call(
        act_kernel,
        out_shape=[jax.ShapeDtypeStruct((GROUPS, HID, GROUP_ROWS), BF16)] * 2
        + [jax.ShapeDtypeStruct(piece.shape, piece.dtype)],
        grid_spec=pltpu.PrefetchScalarGridSpec(
            num_scalar_prefetch=1,
            grid=(N_TILE,),
            in_specs=[
                pl.BlockSpec((1, HID, BLOCK), lambda i, place: (i, 0, 0)),
                pl.BlockSpec(memory_space=pl.ANY),
            ],
            out_specs=[pl.BlockSpec((GROUPS, HID, GROUP_ROWS), lambda i, place: (0, 0, 0), pipeline_mode=pl.Buffered(1))] * 2
            + [pl.BlockSpec(memory_space=pl.ANY)],
            scratch_shapes=[
                pltpu.VMEM((2 * SLOTS, LANES), F32),
                pltpu.VMEM((2 * BLOCK, LANES), F32),
                pltpu.SemaphoreType.DMA(()),
            ],
        ),
        compiler_params=pltpu.CompilerParams(vmem_limit_bytes=17 * 2**20),
        cost_estimate=pl.CostEstimate(flops=0, bytes_accessed=70_000_000, transcendentals=0),
        name="act_rows",
    )(place, act, piece)


def product_kernel(hand_on, weight_ref, *refs):
    pieces = refs[:4]
    if hand_on is None:
        mine_ref, theirs_ref, sums_ref = refs[-3:]
    else:
        mine_ref, theirs_ref, sums_ref, next_ref, sem = refs[-5:]
        copy = pltpu.make_async_copy(pieces[hand_on], next_ref, sem)
        copy.start()
    for k in range(4):
        piece = pieces[k][...]
        term = lax.dot_general(piece, weight_ref[...], (((1,), (1,)), ((), ())), preferred_element_type=F32)
        store_rows(mine_ref, 2 * k * ROWS, term[:, :HID])
        store_rows(theirs_ref, 2 * k * ROWS, term[:, HID:])
        sums_ref[k:k + 1, :] = jnp.sum(piece.astype(F32), axis=0, keepdims=True)
    if hand_on is not None:
        copy.wait()


def products_of(weight, pieces, after, hand_on=None):
    vmem, anywhere = pl.BlockSpec(memory_space=pltpu.VMEM), pl.BlockSpec(memory_space=pl.ANY)
    half = jax.ShapeDtypeStruct((2 * GROUP_ROWS, LANES), F32)
    out = [pltpu.VMEM(half.shape, F32), half, jax.ShapeDtypeStruct((4, WIDTH), F32)]
    return pl.pallas_call(
        functools.partial(product_kernel, hand_on),
        out_shape=out + [jax.ShapeDtypeStruct((ROWS, WIDTH), BF16)] * (hand_on is not None),
        in_specs=[vmem] * 5 + [anywhere] * len(after),
        out_specs=[vmem] * 3 + [anywhere] * (hand_on is not None),
        scratch_shapes=[pltpu.SemaphoreType.DMA(())] * (hand_on is not None),
        compiler_params=pltpu.CompilerParams(vmem_limit_bytes=6 * 2**20),
        cost_estimate=pl.CostEstimate(flops=1_300_000_000, bytes_accessed=8_000_000, transcendentals=0),
        name="products",
    )(weight, *pieces, *after)


def slot_kernel(count, gather_rows, keep, place_ref, blocks_ref, *refs):
    if gather_rows:
        rows_ref, out_ref, picked, sems = refs[-4:] if keep else (refs[-1], *refs[-4:-1])
        copies = [
            pltpu.make_async_copy(refs[k], rows_ref.at[pl.ds(k * 2 * GROUP_ROWS, 2 * GROUP_ROWS), :], sems.at[k])
            for k in range(8)
        ]
        for copy in copies:
            copy.start()
        for copy in copies:
            copy.wait()
    else:
        rows_ref, (out_ref, picked) = refs[0], refs[-2:]

    @pl.loop(0, count)
    def _(b):
        base = blocks_ref[b] * BLOCK

        @pl.loop(0, BLOCK, step=UNROLL)
        def _(start):
            held = []
            for i in range(UNROLL):
                where = pl.multiple_of(place_ref[base + start + i], 2)
                held.append(rows_ref[pl.ds(where, 2), :])
            for i in range(UNROLL):
                picked[pl.ds(pl.multiple_of(2 * start, 2) + 2 * i, 2), :] = held[i]

        left, right = load_turned(picked, 0, BLOCK)
        out_ref[b, 0:LANES, :] = left
        out_ref[b, LANES:HID, :] = right


def to_slot_order(place, blocks, rows, after, keep=False):
    count = blocks.shape[0]
    vmem, anywhere = pl.BlockSpec(memory_space=pltpu.VMEM), pl.BlockSpec(memory_space=pl.ANY)
    out = [pltpu.VMEM((count, HID, BLOCK), F32)]
    whole = len(rows) == 1
    scratch = [pltpu.VMEM((2 * BLOCK, LANES), F32)] + [pltpu.SemaphoreType.DMA((8,))] * (not whole)
    if keep:
        out.insert(0, pltpu.VMEM((2 * SLOTS, LANES), F32))
    elif not whole:
        scratch.append(pltpu.VMEM((2 * SLOTS, LANES), F32))
    return pl.pallas_call(
        functools.partial(slot_kernel, count, not whole, keep),
        out_shape=out,
        in_specs=[pl.BlockSpec(memory_space=pltpu.SMEM)] * 2
        + [vmem if whole else anywhere] * len(rows)
        + [anywhere] * len(after),
        out_specs=[vmem] * len(out),
        scratch_shapes=scratch,
        compiler_params=pltpu.CompilerParams(vmem_limit_bytes=(5 if whole else 50) * 2**20),
        cost_estimate=pl.CostEstimate(flops=0, bytes_accessed=8_000_000 * count, transcendentals=0),
        name="slot_rows",
    )(place, blocks, *rows, *after)


def hop_kernel(which, fresh, terms_ref, come_ref, *refs):
    out_ref = refs[-1]
    term, come = terms_ref[which], come_ref[...].astype(F32)
    if fresh is None:
        out_ref[...] = (term + come).astype(BF16)
        return
    added = slice(HALF, HID) if fresh == 0 else slice(0, HALF)
    out_ref[added, :] = (term[added] + come).astype(BF16)
    out_ref[fresh:fresh + HALF, :] = term[fresh:fresh + HALF].astype(BF16)


def hop(which, fresh, terms, come, after=()):
    vmem = pl.BlockSpec(memory_space=pltpu.VMEM)
    return pl.pallas_call(
        functools.partial(hop_kernel, which, fresh),
        out_shape=jax.ShapeDtypeStruct((HID, BLOCK), BF16),
        in_specs=[vmem] * 2 + [pl.BlockSpec(memory_space=pl.ANY)] * len(after),
        out_specs=vmem,
        compiler_params=pltpu.CompilerParams(vmem_limit_bytes=4 * 2**20),
        cost_estimate=pl.CostEstimate(flops=0, bytes_accessed=1_500_000, transcendentals=0),
        name="hop_sum",
    )(terms, come, *after)


def weight_kernel(group, first, mine_ref, theirs_ref, *refs):
    pieces = refs[:4]
    out_mine, out_theirs, act, held, sems = refs[-5:]
    copies = [
        pltpu.make_async_copy(piece, held.at[pl.ds(k * ROWS, ROWS), :], sems.at[k]) for k, piece in enumerate(pieces)
    ]
    copies.append(pltpu.make_async_copy(mine_ref.at[group], act.at[pl.ds(0, HID), :], sems.at[4]))
    copies.append(pltpu.make_async_copy(theirs_ref.at[group], act.at[pl.ds(HID, HID), :], sems.at[5]))
    for copy in copies:
        copy.start()
    for copy in copies:
        copy.wait()
    for n in range(0, WIDTH, 256):
        columns = slice(n, n + 256)
        term = jnp.dot(act[...], held[:, columns], preferred_element_type=F32)
        out_mine[:, columns] = term[:HID] if first else refs[4][:, columns] + term[:HID]
        out_theirs[:, columns] = term[HID:] if first else refs[5][:, columns] + term[HID:]


def weight_term(group, mine, theirs, pieces, totals, after):
    vmem, anywhere = pl.BlockSpec(memory_space=pltpu.VMEM), pl.BlockSpec(memory_space=pl.ANY)
    return pl.pallas_call(
        functools.partial(weight_kernel, group, not totals),
        out_shape=[jax.ShapeDtypeStruct((HID, WIDTH), F32)] * 2,
        in_specs=[anywhere] * 6 + [vmem] * len(totals) + [anywhere] * len(after),
        out_specs=[vmem] * 2,
        scratch_shapes=[
            pltpu.VMEM((2 * HID, GROUP_ROWS), BF16),
            pltpu.VMEM((GROUP_ROWS, WIDTH), BF16),
            pltpu.SemaphoreType.DMA((6,)),
        ],
        compiler_params=pltpu.CompilerParams(vmem_limit_bytes=6 * 2**20),
        cost_estimate=pl.CostEstimate(flops=1_300_000_000, bytes_accessed=8_000_000, transcendentals=0),
        name="weight_term",
    )(mine, theirs, *pieces, *totals, *after)


def gelu_parts(pre):
    value = pre.astype(F32)
    cdf = 0.5 * (1.0 + jax.scipy.special.erf(value * 0.7071067811865476))
    activated = value * cdf
    slope = cdf + value * jnp.exp(-0.5 * value * value) * 0.3989422804014327
    return activated, slope


def body(grad_seq, positions, pre_act, w_out):
    me = lax.axis_index("text")
    place = 2 * (arrival_place(positions // ROWS, me) * ROWS + positions % ROWS)
    piece_of = arrival_place(jnp.arange(N_TEXT, dtype=jnp.int32), me)

    activated, slope = gelu_parts(pre_act.T)
    act_all = lax.all_gather(activated.astype(BF16), "tile", axis=0)
    swap = lambda value: lax.ppermute(value, "text", SWAP)
    send = lambda value, perm: lax.ppermute(value, "text", perm)
    weight = jnp.concatenate([w_out, swap(w_out)], axis=0)

    got = {(0, 0): grad_seq, (1, 0): send(grad_seq, FIRST_UP), (3, 0): send(grad_seq, FIRST_DOWN)}
    got[0, 1], got[0, 3] = send(grad_seq, SECOND_UP), send(grad_seq, SECOND_DOWN)
    got[2, 0] = send(got[1, 0], FIRST_UP)
    for first in (1, 2):
        got[first, 1], got[first, 3] = send(got[first, 0], SECOND_UP), send(got[first, 0], SECOND_DOWN)
    got[0, 2] = send(got[0, 1], SECOND_UP)
    first_products = products_of(weight, [got[key] for key in ARRIVAL[:4]], [], 2)
    got[3, 1], got[3, 3] = send(first_products[3], SECOND_UP), send(got[3, 0], SECOND_DOWN)
    act_mine, act_theirs, late_piece = act_in_arrival_order(place, act_all, got[3, 3])
    act_theirs = swap(act_theirs)
    mine, theirs, sums = [], [], []
    for g in range(GROUPS):
        pieces = [got[key] for key in ARRIVAL[4 * g:4 * g + 4]]
        kept, sent, part, *handed = first_products if g == 0 else products_of(weight, pieces, [], 1 if g == 1 else None)
        if g == 1:
            got[1, 2] = send(handed[0], SECOND_UP)
            got[3, 2], got[2, 2] = send(late_piece, SECOND_DOWN), send(got[2, 3], SECOND_DOWN)
        mine.append(kept)
        theirs.append(swap(sent))
        sums.append(part)
    groups = [[got[key] for key in ARRIVAL[4 * g:4 * g + 4]] for g in range(GROUPS)]
    tile = lax.axis_index("tile")
    parts = mine + theirs

    def slots(steps, rows, after, keep=False):
        return to_slot_order(place, (tile + jnp.array(steps, jnp.int32)) % N_TILE, rows, after, keep)

    rows, across = slots([4], parts, [], keep=True)
    (middle,) = slots([3, 5, 2, 6], [rows], [across])
    up = lambda value: lax.ppermute(value.astype(BF16), "tile", TILE_UP)
    down = lambda value: lax.ppermute(value.astype(BF16), "tile", TILE_DOWN)
    rise, fall = up(across[0, :HALF]), down(across[0, HALF:])
    (nearest,) = slots([1, 7, 0], parts, [rise])
    rise, fall = up(hop(0, HALF, middle, rise)), down(hop(1, 0, middle, fall))
    arrived = [rise]
    totals = weight_term(0, act_mine, act_theirs, groups[0], [], [])
    totals = weight_term(1, act_mine, act_theirs, groups[1], totals, [])
    sums = jnp.concatenate(sums, axis=0)
    sums = jnp.concatenate([sums, swap(sums)], axis=0)
    grad_bias = jnp.sum(sums[piece_of], axis=0)
    rise, fall = up(hop(2, None, middle, rise, [totals[0], grad_bias])), down(hop(3, None, middle, fall))
    arrived.append(rise)
    rise, fall = up(hop(0, None, nearest, rise)), down(hop(1, None, nearest, fall))
    grad_pre = (nearest[2] + rise.astype(F32) + fall.astype(F32)) * lax.optimization_barrier(slope)
    for g in range(2, GROUPS):
        totals = weight_term(g, act_mine, act_theirs, groups[g], totals, arrived[1:] if g == 2 else [])
    grad_w = totals[0] + swap(totals[1])
    return grad_pre.T, grad_w, grad_bias


def solution(mesh):
    in_specs = (P("text", "tile"), P(), P("tile", "text"), P("text", "tile"))
    out_specs = (P("tile", "text"), P("text", "tile"), P("tile"))
    return jax.shard_map(body, mesh=mesh, in_specs=in_specs, out_specs=out_specs, check_vma=False)
```

```python
import functools

import jax
import jax.numpy as jnp
from jax import lax
from jax.experimental import pallas as pl
from jax.experimental.pallas import tpu as pltpu
from jax.sharding import PartitionSpec as P

SIDE = 4
N_TEXT = 2 * SIDE * SIDE
N_TILE = 8
ROWS = 320
HID = 160
BLOCK = 1280
SLOTS = 10240
WIDTH = 1024
HALF = HID // 2
LANES = 128
GROUPS = 4
GROUP_ROWS = 4 * ROWS
UNROLL = 32
F32 = jnp.float32
BF16 = jnp.bfloat16


def plane_perm(step0, step1):
    pairs = []
    for y in range(SIDE):
        for x in range(SIDE):
            for core, (dy, dx) in ((0, step0), (1, step1)):
                target = (((y + dy) % SIDE) * SIDE + (x + dx) % SIDE) * 2 + core
                pairs.append(((y * SIDE + x) * 2 + core, target))
    return pairs


FIRST_UP = plane_perm((0, 1), (1, 0))
FIRST_DOWN = plane_perm((0, -1), (-1, 0))
SECOND_UP = plane_perm((1, 0), (0, 1))
SECOND_DOWN = plane_perm((-1, 0), (0, -1))
ARRIVAL = [(0, 0), (1, 0), (3, 0), (0, 1), (0, 3), (1, 1), (2, 0), (3, 1), (1, 3), (3, 3), (0, 2), (2, 1), (2, 3), (1, 2), (3, 2), (2, 2)]
SWAP = [(i, i ^ 1) for i in range(N_TEXT)]
TILE_UP = [(i, (i + 1) % N_TILE) for i in range(N_TILE)]
TILE_DOWN = [(i, (i - 1) % N_TILE) for i in range(N_TILE)]


def arrival_place(device, me):
    core, x, y = device & 1, (device >> 1) & 3, device >> 3
    my_core, my_x, my_y = me & 1, (me >> 1) & 3, me >> 3
    dx, dy = (my_x - x) & 3, (my_y - y) & 3
    first = jnp.where(core == 0, dx, dy)
    second = jnp.where(core == 0, dy, dx)
    codes = [sum(ARRIVAL.index((i, j)) << (4 * i) for i in range(SIDE)) for j in range(SIDE)]
    code = jnp.where(second == 0, codes[0], jnp.where(second == 1, codes[1], jnp.where(second == 2, codes[2], codes[3])))
    return (core ^ my_core) * 16 + ((code >> (4 * first)) & 15)


def store_rows(ref, start, value):
    count = value.shape[0]
    ref[pl.ds(start, count, stride=2), :] = value[:, :LANES]
    ref[pl.ds(start + 1, count, stride=2), 0:HID - LANES] = value[:, LANES:]


def load_turned(ref, start, count):
    left = ref[pl.ds(start, count, stride=2), :].T
    right = ref[pl.ds(start + 1, count, stride=2), :].T
    return left, right[0:HID - LANES]


def act_kernel(place_ref, act_ref, piece_ref, mine_ref, theirs_ref, next_ref, rows, turned, sem):
    block = pl.program_id(0)
    copy = pltpu.make_async_copy(piece_ref, next_ref, sem)

    @pl.when(block == 0)
    def _():
        copy.start()

    store_rows(turned, 0, act_ref[0].astype(F32).T)

    @pl.loop(0, BLOCK, step=UNROLL)
    def _(start):
        held = [turned[pl.ds(pl.multiple_of(2 * start, 2) + 2 * i, 2), :] for i in range(UNROLL)]
        for i in range(UNROLL):
            where = pl.multiple_of(place_ref[block * BLOCK + start + i], 2)
            rows[pl.ds(where, 2), :] = held[i]

    @pl.when(block == N_TILE - 1)
    def _():
        for group in range(2 * GROUPS):
            left, right = load_turned(rows, group * 2 * GROUP_ROWS, GROUP_ROWS)
            out_ref = (mine_ref, theirs_ref)[group // GROUPS]
            out_ref[group % GROUPS, 0:LANES, :] = left.astype(BF16)
            out_ref[group % GROUPS, LANES:HID, :] = right.astype(BF16)
        copy.wait()


def act_in_arrival_order(place, act, piece):
    return pl.pallas_call(
        act_kernel,
        out_shape=[jax.ShapeDtypeStruct((GROUPS, HID, GROUP_ROWS), BF16)] * 2
        + [jax.ShapeDtypeStruct(piece.shape, piece.dtype)],
        grid_spec=pltpu.PrefetchScalarGridSpec(
            num_scalar_prefetch=1,
            grid=(N_TILE,),
            in_specs=[
                pl.BlockSpec((1, HID, BLOCK), lambda i, place: (i, 0, 0)),
                pl.BlockSpec(memory_space=pl.ANY),
            ],
            out_specs=[pl.BlockSpec((GROUPS, HID, GROUP_ROWS), lambda i, place: (0, 0, 0), pipeline_mode=pl.Buffered(1))] * 2
            + [pl.BlockSpec(memory_space=pl.ANY)],
            scratch_shapes=[
                pltpu.VMEM((2 * SLOTS, LANES), F32),
                pltpu.VMEM((2 * BLOCK, LANES), F32),
                pltpu.SemaphoreType.DMA(()),
            ],
        ),
        compiler_params=pltpu.CompilerParams(vmem_limit_bytes=17 * 2**20),
        cost_estimate=pl.CostEstimate(flops=0, bytes_accessed=70_000_000, transcendentals=0),
        name="act_rows",
    )(place, act, piece)


def product_kernel(hand_on, weight_ref, *refs):
    pieces = refs[:4]
    if hand_on is None:
        mine_ref, theirs_ref, sums_ref = refs[-3:]
    else:
        mine_ref, theirs_ref, sums_ref, next_ref, sem = refs[-5:]
        copy = pltpu.make_async_copy(pieces[hand_on], next_ref, sem)
        copy.start()
    for k in range(4):
        piece = pieces[k][...]
        term = lax.dot_general(piece, weight_ref[...], (((1,), (1,)), ((), ())), preferred_element_type=F32)
        store_rows(mine_ref, 2 * k * ROWS, term[:, :HID])
        store_rows(theirs_ref, 2 * k * ROWS, term[:, HID:])
        sums_ref[k:k + 1, :] = jnp.sum(piece.astype(F32), axis=0, keepdims=True)
    if hand_on is not None:
        copy.wait()


def products_of(weight, pieces, after, hand_on=None):
    vmem, anywhere = pl.BlockSpec(memory_space=pltpu.VMEM), pl.BlockSpec(memory_space=pl.ANY)
    half = jax.ShapeDtypeStruct((2 * GROUP_ROWS, LANES), F32)
    out = [pltpu.VMEM(half.shape, F32), half, jax.ShapeDtypeStruct((4, WIDTH), F32)]
    return pl.pallas_call(
        functools.partial(product_kernel, hand_on),
        out_shape=out + [jax.ShapeDtypeStruct((ROWS, WIDTH), BF16)] * (hand_on is not None),
        in_specs=[vmem] * 5 + [anywhere] * len(after),
        out_specs=[vmem] * 3 + [anywhere] * (hand_on is not None),
        scratch_shapes=[pltpu.SemaphoreType.DMA(())] * (hand_on is not None),
        compiler_params=pltpu.CompilerParams(vmem_limit_bytes=6 * 2**20),
        cost_estimate=pl.CostEstimate(flops=1_300_000_000, bytes_accessed=8_000_000, transcendentals=0),
        name="products",
    )(weight, *pieces, *after)


def slot_kernel(count, gather_rows, keep, place_ref, blocks_ref, *refs):
    if gather_rows:
        rows_ref, out_ref, picked, sems = refs[-4:] if keep else (refs[-1], *refs[-4:-1])
        copies = [
            pltpu.make_async_copy(refs[k], rows_ref.at[pl.ds(k * 2 * GROUP_ROWS, 2 * GROUP_ROWS), :], sems.at[k])
            for k in range(8)
        ]
        for copy in copies:
            copy.start()
        for copy in copies:
            copy.wait()
    else:
        rows_ref, (out_ref, picked) = refs[0], refs[-2:]

    @pl.loop(0, count)
    def _(b):
        base = blocks_ref[b] * BLOCK

        @pl.loop(0, BLOCK, step=UNROLL)
        def _(start):
            held = []
            for i in range(UNROLL):
                where = pl.multiple_of(place_ref[base + start + i], 2)
                held.append(rows_ref[pl.ds(where, 2), :])
            for i in range(UNROLL):
                picked[pl.ds(pl.multiple_of(2 * start, 2) + 2 * i, 2), :] = held[i]

        left, right = load_turned(picked, 0, BLOCK)
        out_ref[b, 0:LANES, :] = left
        out_ref[b, LANES:HID, :] = right


def to_slot_order(place, blocks, rows, after, keep=False):
    count = blocks.shape[0]
    vmem, anywhere = pl.BlockSpec(memory_space=pltpu.VMEM), pl.BlockSpec(memory_space=pl.ANY)
    out = [pltpu.VMEM((count, HID, BLOCK), F32)]
    whole = len(rows) == 1
    scratch = [pltpu.VMEM((2 * BLOCK, LANES), F32)] + [pltpu.SemaphoreType.DMA((8,))] * (not whole)
    if keep:
        out.insert(0, pltpu.VMEM((2 * SLOTS, LANES), F32))
    elif not whole:
        scratch.append(pltpu.VMEM((2 * SLOTS, LANES), F32))
    return pl.pallas_call(
        functools.partial(slot_kernel, count, not whole, keep),
        out_shape=out,
        in_specs=[pl.BlockSpec(memory_space=pltpu.SMEM)] * 2
        + [vmem if whole else anywhere] * len(rows)
        + [anywhere] * len(after),
        out_specs=[vmem] * len(out),
        scratch_shapes=scratch,
        compiler_params=pltpu.CompilerParams(vmem_limit_bytes=(5 if whole else 50) * 2**20),
        cost_estimate=pl.CostEstimate(flops=0, bytes_accessed=8_000_000 * count, transcendentals=0),
        name="slot_rows",
    )(place, blocks, *rows, *after)


def hop_kernel(which, fresh, terms_ref, come_ref, *refs):
    out_ref = refs[-1]
    term, come = terms_ref[which], come_ref[...].astype(F32)
    if fresh is None:
        out_ref[...] = (term + come).astype(BF16)
        return
    added = slice(HALF, HID) if fresh == 0 else slice(0, HALF)
    out_ref[added, :] = (term[added] + come).astype(BF16)
    out_ref[fresh:fresh + HALF, :] = term[fresh:fresh + HALF].astype(BF16)


def hop(which, fresh, terms, come, after=()):
    vmem = pl.BlockSpec(memory_space=pltpu.VMEM)
    return pl.pallas_call(
        functools.partial(hop_kernel, which, fresh),
        out_shape=jax.ShapeDtypeStruct((HID, BLOCK), BF16),
        in_specs=[vmem] * 2 + [pl.BlockSpec(memory_space=pl.ANY)] * len(after),
        out_specs=vmem,
        compiler_params=pltpu.CompilerParams(vmem_limit_bytes=4 * 2**20),
        cost_estimate=pl.CostEstimate(flops=0, bytes_accessed=1_500_000, transcendentals=0),
        name="hop_sum",
    )(terms, come, *after)


def weight_kernel(group, first, mine_ref, theirs_ref, *refs):
    pieces = refs[:4]
    out_mine, out_theirs, act, held, sems = refs[-5:]
    copies = [
        pltpu.make_async_copy(piece, held.at[pl.ds(k * ROWS, ROWS), :], sems.at[k]) for k, piece in enumerate(pieces)
    ]
    copies.append(pltpu.make_async_copy(mine_ref.at[group], act.at[pl.ds(0, HID), :], sems.at[4]))
    copies.append(pltpu.make_async_copy(theirs_ref.at[group], act.at[pl.ds(HID, HID), :], sems.at[5]))
    for copy in copies:
        copy.start()
    for copy in copies:
        copy.wait()
    for n in range(0, WIDTH, 256):
        columns = slice(n, n + 256)
        term = jnp.dot(act[...], held[:, columns], preferred_element_type=F32)
        out_mine[:, columns] = term[:HID] if first else refs[4][:, columns] + term[:HID]
        out_theirs[:, columns] = term[HID:] if first else refs[5][:, columns] + term[HID:]


def weight_term(group, mine, theirs, pieces, totals, after):
    vmem, anywhere = pl.BlockSpec(memory_space=pltpu.VMEM), pl.BlockSpec(memory_space=pl.ANY)
    return pl.pallas_call(
        functools.partial(weight_kernel, group, not totals),
        out_shape=[jax.ShapeDtypeStruct((HID, WIDTH), F32)] * 2,
        in_specs=[anywhere] * 6 + [vmem] * len(totals) + [anywhere] * len(after),
        out_specs=[vmem] * 2,
        scratch_shapes=[
            pltpu.VMEM((2 * HID, GROUP_ROWS), BF16),
            pltpu.VMEM((GROUP_ROWS, WIDTH), BF16),
            pltpu.SemaphoreType.DMA((6,)),
        ],
        compiler_params=pltpu.CompilerParams(vmem_limit_bytes=6 * 2**20),
        cost_estimate=pl.CostEstimate(flops=1_300_000_000, bytes_accessed=8_000_000, transcendentals=0),
        name="weight_term",
    )(mine, theirs, *pieces, *totals, *after)


def bias_kernel(order_ref, mine_ref, theirs_ref, out_ref, held, ordered):
    held[0:16, :] = mine_ref[...]
    held[16:32, :] = theirs_ref[...]
    for device in range(N_TEXT):
        ordered[device:device + 1, :] = held[pl.ds(order_ref[device], 1), :]
    out_ref[...] = jnp.sum(ordered[...], axis=0, keepdims=True)


def bias_sum(order, mine, theirs):
    vmem = pl.BlockSpec(memory_space=pltpu.VMEM)
    return pl.pallas_call(
        bias_kernel,
        out_shape=jax.ShapeDtypeStruct((1, WIDTH), F32),
        in_specs=[pl.BlockSpec(memory_space=pltpu.SMEM), vmem, vmem],
        out_specs=vmem,
        scratch_shapes=[pltpu.VMEM((N_TEXT, WIDTH), F32)] * 2,
        compiler_params=pltpu.CompilerParams(vmem_limit_bytes=2 * 2**20),
        cost_estimate=pl.CostEstimate(flops=0, bytes_accessed=1_000_000, transcendentals=0),
        name="bias_sum",
    )(order, mine, theirs)[0]


def gelu_parts(pre):
    value = pre.astype(F32)
    cdf = 0.5 * (1.0 + jax.scipy.special.erf(value * 0.7071067811865476))
    activated = value * cdf
    slope = cdf + value * jnp.exp(-0.5 * value * value) * 0.3989422804014327
    return activated, slope


def body(grad_seq, positions, pre_act, w_out):
    me = lax.axis_index("text")
    place = 2 * (arrival_place(positions // ROWS, me) * ROWS + positions % ROWS)
    piece_of = arrival_place(jnp.arange(N_TEXT, dtype=jnp.int32), me)

    activated, slope = gelu_parts(pre_act.T)
    act_all = lax.all_gather(activated.astype(BF16), "tile", axis=0)
    swap = lambda value: lax.ppermute(value, "text", SWAP)
    send = lambda value, perm: lax.ppermute(value, "text", perm)
    weight = jnp.concatenate([w_out, swap(w_out)], axis=0)

    got = {(0, 0): grad_seq, (1, 0): send(grad_seq, FIRST_UP), (3, 0): send(grad_seq, FIRST_DOWN)}
    got[0, 1], got[0, 3] = send(grad_seq, SECOND_UP), send(grad_seq, SECOND_DOWN)
    got[2, 0] = send(got[1, 0], FIRST_UP)
    for first in (1, 2):
        got[first, 1], got[first, 3] = send(got[first, 0], SECOND_UP), send(got[first, 0], SECOND_DOWN)
    got[0, 2] = send(got[0, 1], SECOND_UP)
    first_products = products_of(weight, [got[key] for key in ARRIVAL[:4]], [], 2)
    got[3, 1], got[3, 3] = send(first_products[3], SECOND_UP), send(got[3, 0], SECOND_DOWN)
    act_mine, act_theirs, late_piece = act_in_arrival_order(place, act_all, got[3, 3])
    act_theirs = swap(act_theirs)
    mine, theirs, sums = [], [], []
    for g in range(GROUPS):
        pieces = [got[key] for key in ARRIVAL[4 * g:4 * g + 4]]
        kept, sent, part, *handed = first_products if g == 0 else products_of(weight, pieces, [], 1 if g == 1 else None)
        if g == 1:
            got[1, 2] = send(handed[0], SECOND_UP)
            got[3, 2], got[2, 2] = send(late_piece, SECOND_DOWN), send(got[2, 3], SECOND_DOWN)
        mine.append(kept)
        theirs.append(swap(sent))
        sums.append(part)
    groups = [[got[key] for key in ARRIVAL[4 * g:4 * g + 4]] for g in range(GROUPS)]
    tile = lax.axis_index("tile")
    parts = mine + theirs

    def slots(steps, rows, after, keep=False):
        return to_slot_order(place, (tile + jnp.array(steps, jnp.int32)) % N_TILE, rows, after, keep)

    rows, across = slots([4], parts, [], keep=True)
    (middle,) = slots([3, 5, 2, 6], [rows], [across])
    up = lambda value: lax.ppermute(value.astype(BF16), "tile", TILE_UP)
    down = lambda value: lax.ppermute(value.astype(BF16), "tile", TILE_DOWN)
    rise, fall = up(across[0, :HALF]), down(across[0, HALF:])
    (nearest,) = slots([1, 7, 0], parts, [rise])
    rise, fall = up(hop(0, HALF, middle, rise)), down(hop(1, 0, middle, fall))
    arrived = [rise]
    totals = weight_term(0, act_mine, act_theirs, groups[0], [], [])
    totals = weight_term(1, act_mine, act_theirs, groups[1], totals, [])
    rise, fall = up(hop(2, None, middle, rise, totals[:1])), down(hop(3, None, middle, fall))
    arrived.append(rise)
    rise, fall = up(hop(0, None, nearest, rise)), down(hop(1, None, nearest, fall))
    grad_pre = (nearest[2] + rise.astype(F32) + fall.astype(F32)) * lax.optimization_barrier(slope)
    for g in range(2, GROUPS):
        totals = weight_term(g, act_mine, act_theirs, groups[g], totals, arrived[1:] if g == 2 else [])
    grad_w = totals[0] + swap(totals[1])
    sums = jnp.concatenate(sums, axis=0)
    grad_bias = bias_sum(piece_of, sums, swap(sums))
    return grad_pre.T, grad_w, grad_bias


def solution(mesh):
    in_specs = (P("text", "tile"), P(), P("tile", "text"), P("text", "tile"))
    out_specs = (P("tile", "text"), P("text", "tile"), P("tile"))
    return jax.shard_map(body, mesh=mesh, in_specs=in_specs, out_specs=out_specs, check_vma=False)
```

```python
import functools

import jax
import jax.numpy as jnp
from jax import lax
from jax.experimental import pallas as pl
from jax.experimental.pallas import tpu as pltpu
from jax.sharding import PartitionSpec as P

SIDE = 4
N_TEXT = 2 * SIDE * SIDE
N_TILE = 8
ROWS = 320
HID = 160
BLOCK = 1280
SLOTS = 10240
WIDTH = 1024
HALF = HID // 2
LANES = 128
GROUPS = 4
GROUP_ROWS = 4 * ROWS
UNROLL = 32
F32 = jnp.float32
BF16 = jnp.bfloat16


def plane_perm(step0, step1):
    pairs = []
    for y in range(SIDE):
        for x in range(SIDE):
            for core, (dy, dx) in ((0, step0), (1, step1)):
                target = (((y + dy) % SIDE) * SIDE + (x + dx) % SIDE) * 2 + core
                pairs.append(((y * SIDE + x) * 2 + core, target))
    return pairs


FIRST_UP = plane_perm((0, 1), (1, 0))
FIRST_DOWN = plane_perm((0, -1), (-1, 0))
SECOND_UP = plane_perm((1, 0), (0, 1))
SECOND_DOWN = plane_perm((-1, 0), (0, -1))
ARRIVAL = [(0, 0), (1, 0), (3, 0), (0, 1), (0, 3), (1, 1), (2, 0), (3, 1), (1, 3), (3, 3), (0, 2), (2, 1), (2, 3), (1, 2), (3, 2), (2, 2)]
SWAP = [(i, i ^ 1) for i in range(N_TEXT)]
TILE_UP = [(i, (i + 1) % N_TILE) for i in range(N_TILE)]
TILE_DOWN = [(i, (i - 1) % N_TILE) for i in range(N_TILE)]


def arrival_place(device, me):
    core, x, y = device & 1, (device >> 1) & 3, device >> 3
    my_core, my_x, my_y = me & 1, (me >> 1) & 3, me >> 3
    dx, dy = (my_x - x) & 3, (my_y - y) & 3
    first = jnp.where(core == 0, dx, dy)
    second = jnp.where(core == 0, dy, dx)
    codes = [sum(ARRIVAL.index((i, j)) << (4 * i) for i in range(SIDE)) for j in range(SIDE)]
    code = jnp.where(second == 0, codes[0], jnp.where(second == 1, codes[1], jnp.where(second == 2, codes[2], codes[3])))
    return (core ^ my_core) * 16 + ((code >> (4 * first)) & 15)


def store_rows(ref, start, value):
    count = value.shape[0]
    ref[pl.ds(start, count, stride=2), :] = value[:, :LANES]
    ref[pl.ds(start + 1, count, stride=2), 0:HID - LANES] = value[:, LANES:]


def load_turned(ref, start, count):
    left = ref[pl.ds(start, count, stride=2), :].T
    right = ref[pl.ds(start + 1, count, stride=2), :].T
    return left, right[0:HID - LANES]


def act_kernel(place_ref, act_ref, piece_ref, mine_ref, theirs_ref, next_ref, rows, turned, sem):
    block = pl.program_id(0)
    copy = pltpu.make_async_copy(piece_ref, next_ref, sem)

    @pl.when(block == 0)
    def _():
        copy.start()

    store_rows(turned, 0, act_ref[0].astype(F32).T)

    @pl.loop(0, BLOCK, step=UNROLL)
    def _(start):
        held = [turned[pl.ds(pl.multiple_of(2 * start, 2) + 2 * i, 2), :] for i in range(UNROLL)]
        for i in range(UNROLL):
            where = pl.multiple_of(place_ref[block * BLOCK + start + i], 2)
            rows[pl.ds(where, 2), :] = held[i]

    @pl.when(block == N_TILE - 1)
    def _():
        for group in range(2 * GROUPS):
            left, right = load_turned(rows, group * 2 * GROUP_ROWS, GROUP_ROWS)
            out_ref = (mine_ref, theirs_ref)[group // GROUPS]
            out_ref[group % GROUPS, 0:LANES, :] = left.astype(BF16)
            out_ref[group % GROUPS, LANES:HID, :] = right.astype(BF16)
        copy.wait()


def act_in_arrival_order(place, act, piece):
    return pl.pallas_call(
        act_kernel,
        out_shape=[jax.ShapeDtypeStruct((GROUPS, HID, GROUP_ROWS), BF16)] * 2
        + [jax.ShapeDtypeStruct(piece.shape, piece.dtype)],
        grid_spec=pltpu.PrefetchScalarGridSpec(
            num_scalar_prefetch=1,
            grid=(N_TILE,),
            in_specs=[
                pl.BlockSpec((1, HID, BLOCK), lambda i, place: (i, 0, 0)),
                pl.BlockSpec(memory_space=pl.ANY),
            ],
            out_specs=[pl.BlockSpec((GROUPS, HID, GROUP_ROWS), lambda i, place: (0, 0, 0), pipeline_mode=pl.Buffered(1))] * 2
            + [pl.BlockSpec(memory_space=pl.ANY)],
            scratch_shapes=[
                pltpu.VMEM((2 * SLOTS, LANES), F32),
                pltpu.VMEM((2 * BLOCK, LANES), F32),
                pltpu.SemaphoreType.DMA(()),
            ],
        ),
        compiler_params=pltpu.CompilerParams(vmem_limit_bytes=17 * 2**20),
        cost_estimate=pl.CostEstimate(flops=0, bytes_accessed=70_000_000, transcendentals=0),
        name="act_rows",
    )(place, act, piece)


def product_kernel(hand_on, weight_ref, *refs):
    pieces = refs[:4]
    if hand_on is None:
        mine_ref, theirs_ref, sums_ref = refs[-3:]
    else:
        mine_ref, theirs_ref, sums_ref, next_ref, sem = refs[-5:]
        copy = pltpu.make_async_copy(pieces[hand_on], next_ref, sem)
        copy.start()
    for k in range(4):
        piece = pieces[k][...]
        term = lax.dot_general(piece, weight_ref[...], (((1,), (1,)), ((), ())), preferred_element_type=F32)
        store_rows(mine_ref, 2 * k * ROWS, term[:, :HID])
        store_rows(theirs_ref, 2 * k * ROWS, term[:, HID:])
        sums_ref[k:k + 1, :] = jnp.sum(piece.astype(F32), axis=0, keepdims=True)
    if hand_on is not None:
        copy.wait()


def products_of(weight, pieces, after, hand_on=None):
    vmem, anywhere = pl.BlockSpec(memory_space=pltpu.VMEM), pl.BlockSpec(memory_space=pl.ANY)
    half = jax.ShapeDtypeStruct((2 * GROUP_ROWS, LANES), F32)
    out = [pltpu.VMEM(half.shape, F32), half, jax.ShapeDtypeStruct((4, WIDTH), F32)]
    return pl.pallas_call(
        functools.partial(product_kernel, hand_on),
        out_shape=out + [jax.ShapeDtypeStruct((ROWS, WIDTH), BF16)] * (hand_on is not None),
        in_specs=[vmem] * 5 + [anywhere] * len(after),
        out_specs=[vmem] * 3 + [anywhere] * (hand_on is not None),
        scratch_shapes=[pltpu.SemaphoreType.DMA(())] * (hand_on is not None),
        compiler_params=pltpu.CompilerParams(vmem_limit_bytes=6 * 2**20),
        cost_estimate=pl.CostEstimate(flops=1_300_000_000, bytes_accessed=8_000_000, transcendentals=0),
        name="products",
    )(weight, *pieces, *after)


def slot_kernel(count, gather_rows, keep, place_ref, blocks_ref, *refs):
    if gather_rows:
        rows_ref, out_ref, picked, sems = refs[-4:] if keep else (refs[-1], *refs[-4:-1])
        copies = [
            pltpu.make_async_copy(refs[k], rows_ref.at[pl.ds(k * 2 * GROUP_ROWS, 2 * GROUP_ROWS), :], sems.at[k])
            for k in range(8)
        ]
        for copy in copies:
            copy.start()
        for copy in copies:
            copy.wait()
    else:
        rows_ref, (out_ref, picked) = refs[0], refs[-2:]

    @pl.loop(0, count)
    def _(b):
        base = blocks_ref[b] * BLOCK

        @pl.loop(0, BLOCK, step=UNROLL)
        def _(start):
            held = []
            for i in range(UNROLL):
                where = pl.multiple_of(place_ref[base + start + i], 2)
                held.append(rows_ref[pl.ds(where, 2), :])
            for i in range(UNROLL):
                picked[pl.ds(pl.multiple_of(2 * start, 2) + 2 * i, 2), :] = held[i]

        left, right = load_turned(picked, 0, BLOCK)
        out_ref[b, 0:LANES, :] = left
        out_ref[b, LANES:HID, :] = right


def to_slot_order(place, blocks, rows, after, keep=False):
    count = blocks.shape[0]
    vmem, anywhere = pl.BlockSpec(memory_space=pltpu.VMEM), pl.BlockSpec(memory_space=pl.ANY)
    out = [pltpu.VMEM((count, HID, BLOCK), F32)]
    whole = len(rows) == 1
    scratch = [pltpu.VMEM((2 * BLOCK, LANES), F32)] + [pltpu.SemaphoreType.DMA((8,))] * (not whole)
    if keep:
        out.insert(0, pltpu.VMEM((2 * SLOTS, LANES), F32))
    elif not whole:
        scratch.append(pltpu.VMEM((2 * SLOTS, LANES), F32))
    return pl.pallas_call(
        functools.partial(slot_kernel, count, not whole, keep),
        out_shape=out,
        in_specs=[pl.BlockSpec(memory_space=pltpu.SMEM)] * 2
        + [vmem if whole else anywhere] * len(rows)
        + [anywhere] * len(after),
        out_specs=[vmem] * len(out),
        scratch_shapes=scratch,
        compiler_params=pltpu.CompilerParams(vmem_limit_bytes=(5 if whole else 50) * 2**20),
        cost_estimate=pl.CostEstimate(flops=0, bytes_accessed=8_000_000 * count, transcendentals=0),
        name="slot_rows",
    )(place, blocks, *rows, *after)


def hop_kernel(which, fresh, terms_ref, come_ref, *refs):
    out_ref = refs[-1]
    term, come = terms_ref[which], come_ref[...].astype(F32)
    if fresh is None:
        out_ref[...] = (term + come).astype(BF16)
        return
    added = slice(HALF, HID) if fresh == 0 else slice(0, HALF)
    out_ref[added, :] = (term[added] + come).astype(BF16)
    out_ref[fresh:fresh + HALF, :] = term[fresh:fresh + HALF].astype(BF16)


def hop(which, fresh, terms, come, after=()):
    vmem = pl.BlockSpec(memory_space=pltpu.VMEM)
    return pl.pallas_call(
        functools.partial(hop_kernel, which, fresh),
        out_shape=jax.ShapeDtypeStruct((HID, BLOCK), BF16),
        in_specs=[vmem] * 2 + [pl.BlockSpec(memory_space=pl.ANY)] * len(after),
        out_specs=vmem,
        compiler_params=pltpu.CompilerParams(vmem_limit_bytes=4 * 2**20),
        cost_estimate=pl.CostEstimate(flops=0, bytes_accessed=1_500_000, transcendentals=0),
        name="hop_sum",
    )(terms, come, *after)


def weight_kernel(group, first, mine_ref, theirs_ref, *refs):
    pieces = refs[:4]
    out_mine, out_theirs, act, held, sems = refs[-5:]
    copies = [
        pltpu.make_async_copy(piece, held.at[pl.ds(k * ROWS, ROWS), :], sems.at[k]) for k, piece in enumerate(pieces)
    ]
    copies.append(pltpu.make_async_copy(mine_ref.at[group], act.at[pl.ds(0, HID), :], sems.at[4]))
    copies.append(pltpu.make_async_copy(theirs_ref.at[group], act.at[pl.ds(HID, HID), :], sems.at[5]))
    for copy in copies:
        copy.start()
    for copy in copies:
        copy.wait()
    for n in range(0, WIDTH, 256):
        columns = slice(n, n + 256)
        term = jnp.dot(act[...], held[:, columns], preferred_element_type=F32)
        out_mine[:, columns] = term[:HID] if first else refs[4][:, columns] + term[:HID]
        out_theirs[:, columns] = term[HID:] if first else refs[5][:, columns] + term[HID:]


def weight_term(group, mine, theirs, pieces, totals, after):
    vmem, anywhere = pl.BlockSpec(memory_space=pltpu.VMEM), pl.BlockSpec(memory_space=pl.ANY)
    return pl.pallas_call(
        functools.partial(weight_kernel, group, not totals),
        out_shape=[jax.ShapeDtypeStruct((HID, WIDTH), F32)] * 2,
        in_specs=[anywhere] * 6 + [vmem] * len(totals) + [anywhere] * len(after),
        out_specs=[vmem] * 2,
        scratch_shapes=[
            pltpu.VMEM((2 * HID, GROUP_ROWS), BF16),
            pltpu.VMEM((GROUP_ROWS, WIDTH), BF16),
            pltpu.SemaphoreType.DMA((6,)),
        ],
        compiler_params=pltpu.CompilerParams(vmem_limit_bytes=6 * 2**20),
        cost_estimate=pl.CostEstimate(flops=1_300_000_000, bytes_accessed=8_000_000, transcendentals=0),
        name="weight_term",
    )(mine, theirs, *pieces, *totals, *after)


def bias_kernel(order_ref, mine_ref, theirs_ref, out_ref, held, ordered):
    held[0:16, :] = mine_ref[...]
    held[16:32, :] = theirs_ref[...]
    for device in range(N_TEXT):
        ordered[device:device + 1, :] = held[pl.ds(order_ref[device], 1), :]
    out_ref[...] = jnp.sum(ordered[...], axis=0, keepdims=True)


def bias_sum(order, mine, theirs):
    vmem = pl.BlockSpec(memory_space=pltpu.VMEM)
    return pl.pallas_call(
        bias_kernel,
        out_shape=jax.ShapeDtypeStruct((1, WIDTH), F32),
        in_specs=[pl.BlockSpec(memory_space=pltpu.SMEM), vmem, vmem],
        out_specs=vmem,
        scratch_shapes=[pltpu.VMEM((N_TEXT, WIDTH), F32)] * 2,
        compiler_params=pltpu.CompilerParams(vmem_limit_bytes=2 * 2**20),
        cost_estimate=pl.CostEstimate(flops=0, bytes_accessed=1_000_000, transcendentals=0),
        name="bias_sum",
    )(order, mine, theirs)[0]


def gelu_parts(pre):
    value = pre.astype(F32)
    cdf = 0.5 * (1.0 + jax.scipy.special.erf(value * 0.7071067811865476))
    activated = value * cdf
    slope = cdf + value * jnp.exp(-0.5 * value * value) * 0.3989422804014327
    return activated, slope


def body(grad_seq, positions, pre_act, w_out):
    me = lax.axis_index("text")
    place = 2 * (arrival_place(positions // ROWS, me) * ROWS + positions % ROWS)
    piece_of = arrival_place(jnp.arange(N_TEXT, dtype=jnp.int32), me)

    activated, slope = gelu_parts(pre_act.T)
    act_all = lax.all_gather(activated.astype(BF16), "tile", axis=0)
    swap = lambda value: lax.ppermute(value, "text", SWAP)
    send = lambda value, perm: lax.ppermute(value, "text", perm)
    weight = jnp.concatenate([w_out, swap(w_out)], axis=0)

    got = {(0, 0): grad_seq, (1, 0): send(grad_seq, FIRST_UP), (3, 0): send(grad_seq, FIRST_DOWN)}
    got[0, 1], got[0, 3] = send(grad_seq, SECOND_UP), send(grad_seq, SECOND_DOWN)
    got[2, 0] = send(got[1, 0], FIRST_UP)
    for first in (1, 2):
        got[first, 1], got[first, 3] = send(got[first, 0], SECOND_UP), send(got[first, 0], SECOND_DOWN)
    got[0, 2] = send(got[0, 1], SECOND_UP)
    first_products = products_of(weight, [got[key] for key in ARRIVAL[:4]], [], 2)
    got[3, 1], got[3, 3] = send(first_products[3], SECOND_UP), send(got[3, 0], SECOND_DOWN)
    act_mine, act_theirs, late_piece = act_in_arrival_order(place, act_all, got[3, 3])
    act_theirs = swap(act_theirs)
    mine, theirs, sums = [], [], []
    for g in range(GROUPS):
        pieces = [got[key] for key in ARRIVAL[4 * g:4 * g + 4]]
        kept, sent, part, *handed = first_products if g == 0 else products_of(
            weight, pieces, [act_theirs] if g == GROUPS - 1 else [], 1 if g == 1 else None
        )
        if g == 1:
            got[1, 2] = send(handed[0], SECOND_UP)
            got[3, 2], got[2, 2] = send(late_piece, SECOND_DOWN), send(got[2, 3], SECOND_DOWN)
        mine.append(kept)
        theirs.append(swap(sent))
        sums.append(part)
    groups = [[got[key] for key in ARRIVAL[4 * g:4 * g + 4]] for g in range(GROUPS)]
    tile = lax.axis_index("tile")
    parts = mine + theirs

    def slots(steps, rows, after, keep=False):
        return to_slot_order(place, (tile + jnp.array(steps, jnp.int32)) % N_TILE, rows, after, keep)

    rows, across = slots([4], parts, [], keep=True)
    (middle,) = slots([3, 5, 2, 6], [rows], [across])
    up = lambda value: lax.ppermute(value.astype(BF16), "tile", TILE_UP)
    down = lambda value: lax.ppermute(value.astype(BF16), "tile", TILE_DOWN)
    rise, fall = up(across[0, :HALF]), down(across[0, HALF:])
    (nearest,) = slots([1, 7, 0], parts, [rise])
    rise, fall = up(hop(0, HALF, middle, rise)), down(hop(1, 0, middle, fall))
    arrived = [rise]
    totals = weight_term(0, act_mine, act_theirs, groups[0], [], [])
    totals = weight_term(1, act_mine, act_theirs, groups[1], totals, [])
    rise, fall = up(hop(2, None, middle, rise, totals[:1])), down(hop(3, None, middle, fall))
    arrived.append(rise)
    rise, fall = up(hop(0, None, nearest, rise)), down(hop(1, None, nearest, fall))
    grad_pre = (nearest[2] + rise.astype(F32) + fall.astype(F32)) * lax.optimization_barrier(slope)
    for g in range(2, GROUPS):
        totals = weight_term(g, act_mine, act_theirs, groups[g], totals, arrived[1:] if g == 2 else [])
    grad_w = totals[0] + swap(totals[1])
    sums = jnp.concatenate(sums, axis=0)
    grad_bias = bias_sum(piece_of, sums, swap(sums))
    return grad_pre.T, grad_w, grad_bias


def solution(mesh):
    in_specs = (P("text", "tile"), P(), P("tile", "text"), P("text", "tile"))
    out_specs = (P("tile", "text"), P("text", "tile"), P("tile"))
    return jax.shard_map(body, mesh=mesh, in_specs=in_specs, out_specs=out_specs, check_vma=False)
```
